256 devices in a mesh: pass: 16 (over x, y), list: 16 (over z, core).
Axes of the slice: x: 4, y: 4, z: 8, core: 2. Of those that a mesh axis runs over, the one named last changes fastest.
Arguments:
- passages: bfloat16 [49152, 768], P('pass'), may hold values from -11 to 11
- centroids: bfloat16 [12288, 768], P('list'), may hold values from -0.21875 to 0.21875
Outputs:
- new_centroids: float32 [768, 12288], P('pass', 'list')
- list_potential: float32 [12288], P('list')
- passage_potential: float32 [49152], P('pass')
The draws below stay inside these ranges and needn't reach their ends.
All inputs are finite; a program needn't handle non-finite values.
Results may differ from the reference program's by a relative error of at most 0.0023.
Values sent between devices are 32-bit elements; how exact they have to be, the bound alone decides.
A program may use at most 64 MiB of HBM per device.

```python
import math
import jax
import jax.numpy as jnp
from jax import lax

D = 768
ITERS = 4
ROWS = 49152
K = 12288
N_LIST = 16


def draw_passages(key, part):
    key = jax.random.fold_in(key, 11)
    first = jax.random.fold_in(key, 0)
    values = jnp.clip(jax.random.normal(first, (ROWS, D), jnp.float32), -5.5, 5.5)
    return values.astype(jnp.bfloat16)


def level_of(stream_key, dims, cuts, smallest, top_value):
    factor_of = 1.0
    for dim, blocks in cuts:
        heights = jax.random.uniform(jax.random.fold_in(jax.random.fold_in(stream_key, 6), dim), (blocks,), jnp.float32, smallest / len(cuts), top_value / len(cuts))
        factor_of = factor_of * jnp.repeat(jnp.exp(heights), dims[dim] // blocks).reshape((-1,) + (1,) * (len(dims) - 1 - dim))
    return factor_of


def gaussian(key, shape, deviation, reach, pieces=(), held_as=jnp.bfloat16):
    values = jax.random.normal(key, shape, jnp.float32) * deviation
    if len(pieces) > 0:
        values = level_of(key, shape, pieces, -0.22, 0.18) * values
    return jnp.clip(values, min=-reach, max=reach).astype(held_as)


def setup_inputs(seed: int = 0) -> dict:
    arg_keys = jax.random.split(jax.random.key(seed), 3)
    passages = draw_passages(jax.random.fold_in(arg_keys[2], 71), 0)
    centroids = gaussian(arg_keys[1], (K, D), D ** -0.5, 0.21875, ((0, 16),))
    return {"passages": passages, "centroids": centroids}


inv_temp = 20.0


def reference(passages, centroids):
    count_rows = passages.shape[0]
    count_lists = centroids.shape[0]
    width = count_lists // N_LIST
    blocks = centroids.reshape(N_LIST, width, D)
    logshare = math.log(count_rows / count_lists)

    def logit_tile(block):
        return lax.dot_general(passages, block, (((1,), (1,)), ((), ())), preferred_element_type=jnp.float32) * inv_temp

    row_pot = jnp.zeros((count_rows,), jnp.float32)
    col_pot = jnp.zeros((count_lists,), jnp.float32)
    for step in range(ITERS):
        def sweep(carry, block):
            run_max, run_sum = carry
            tile = logit_tile(block)
            shifted = tile + row_pot[:, None]
            col_max = jnp.max(shifted, axis=0)
            col = logshare - (col_max + jnp.log(jnp.sum(jnp.exp(shifted - col_max[None, :]), axis=0)))
            moved = tile + col[None, :]
            new_max = jnp.maximum(run_max, jnp.max(moved, axis=1))
            run_sum = run_sum * jnp.exp(run_max - new_max) + jnp.sum(jnp.exp(moved - new_max[:, None]), axis=1)
            return (new_max, run_sum), col

        start = (jnp.full((count_rows,), -jnp.inf, jnp.float32), jnp.zeros((count_rows,), jnp.float32))
        (run_max, run_sum), cols = lax.scan(sweep, start, blocks)
        row_pot = -(run_max + jnp.log(run_sum))
        col_pot = cols.reshape(count_lists)

    def update(carry, pair):
        block, col = pair
        tile = logit_tile(block)
        plan = jnp.exp(tile + row_pot[:, None] + col[None, :])
        mass = jnp.sum(plan, axis=0)
        weights = plan.astype(jnp.bfloat16)
        sums = lax.dot_general(passages, weights, (((0,), (0,)), ((), ())), preferred_element_type=jnp.float32)
        return carry, sums / mass[None, :]

    unused, parts = lax.scan(update, jnp.zeros((), jnp.float32), (blocks, col_pot.reshape(N_LIST, width)))
    new_centroids = jnp.transpose(parts, (1, 0, 2)).reshape(D, count_lists)
    return new_centroids, col_pot, row_pot
```

```python
import functools
import math

import jax
import jax.numpy as jnp
from jax import lax
from jax.experimental import pallas as pl
from jax.experimental.pallas import tpu as pltpu
from jax.sharding import PartitionSpec as P

ITERS = 4
INV_TEMP = 20.0
LOG2E = math.log2(math.e)
LN2 = math.log(2.0)
F32 = jnp.float32
BF16 = jnp.bfloat16
MESH = pl.DeviceIdType.MESH
CHUNK = 512
GROUP = 256
LINKS = (4, 12, 1, 3)
ORDERS = ((0, 1, 2, 3), (1, 0, 3, 2), (2, 3, 0, 1), (3, 2, 1, 0))


def flip(index, bits):
    out = index
    b = 1
    while b <= bits:
        if bits & b:
            out = out + b * (1 - 2 * ((index // b) % 2))
        b *= 2
    return out


def place_of(order):
    first = order[0]
    axis_bits = lambda seq, unit: [0, unit * seq[1], unit * seq[0], unit * (seq[0] ^ seq[1])]
    low = {0: 1, 1: 3, 2: 1, 3: 3}
    unit = {0: 4, 1: 4, 2: 1, 3: 1}
    major = axis_bits((low[order[0]], low[order[1]]), unit[first])
    minor = axis_bits((low[order[2]], low[order[3]]), unit[order[2]])
    return [a + b for a in major for b in minor]


PLACES = [place_of(order) for order in ORDERS]


def tree(values, op):
    while len(values) > 1:
        values = [op(values[i], values[i + 1]) for i in range(0, len(values), 2)]
    return values[0]


def lse2(values):
    top = tree(values, jnp.maximum)
    total = tree([jnp.exp2(v - top) for v in values], lax.add)
    return top + jnp.log(total) * LOG2E


def kernel(
    share,
    pas_hbm, cen_hbm,
    out_ref, cp_ref, rp_ref,
    cen, pas, tile, pas_t, wts, stag, rb0, rb1, rb2, rb3,
    lane_a, lane_b, csrc, cslot, rsrc, rpair, rmid, rslot, u_ref, w_ref, m_ref,
    in_sem, cs, cr, ps, pr, zs, zr, ss, sr,
):
    rows, depth = pas.shape
    lists = cen.shape[0]
    nrow, ncol = rows // 128, lists // 128
    p, l = lax.axis_index("pass"), lax.axis_index("list")
    rbs = (rb0, rb1, rb2, rb3)

    loads = [pltpu.make_async_copy(cen_hbm, cen, in_sem.at[0])]
    for b in range(rows // CHUNK):
        part = pl.ds(b * CHUNK, CHUNK)
        loads.append(pltpu.make_async_copy(pas_hbm.at[part], pas.at[part], in_sem.at[b + 1]))
    for load in loads:
        load.start()

    barrier = pltpu.get_barrier_semaphore()
    for k in range(1, 16):
        pl.semaphore_signal(barrier, inc=1, device_id=(flip(p, k), l), device_id_type=MESH)
    for k in (1, 2, 4, 6, 8, 10, 12, 14):
        pl.semaphore_signal(barrier, inc=1, device_id=(p, flip(l, k)), device_id_type=MESH)

    def col_send(i):
        for k in range(1, 16):
            pltpu.make_async_remote_copy(
                src_ref=csrc.at[i], dst_ref=cslot.at[i, k - 1], send_sem=cs, recv_sem=cr.at[i],
                device_id=(flip(p, k), l), device_id_type=MESH,
            ).start()

    def col_recv(i):
        pltpu.make_async_copy(cslot.at[i], cslot.at[i], cr.at[i]).wait()
        return [csrc[i]] + [cslot[i, k] for k in range(15)]

    def row_exchange(i, combine):
        copy = pltpu.make_async_remote_copy(
            src_ref=rsrc.at[i], dst_ref=rpair.at[i], send_sem=ps, recv_sem=pr.at[i],
            device_id=(p, flip(l, 1)), device_id_type=MESH,
        )
        copy.start()
        copy.wait_recv()
        rmid[i] = combine([rsrc[i], rpair[i]])
        for k in range(1, 8):
            pltpu.make_async_remote_copy(
                src_ref=rmid.at[i], dst_ref=rslot.at[i, k - 1], send_sem=zs, recv_sem=zr.at[i],
                device_id=(p, flip(l, 2 * k)), device_id_type=MESH,
            ).start()
        pltpu.make_async_copy(rslot.at[i], rslot.at[i], zr.at[i]).wait()
        return combine([rmid[i]] + [rslot[i, k] for k in range(7)])

    def spread(values):
        for k in range(ncol):
            lane_b[k * 128:(k + 1) * 128, :] = jnp.broadcast_to(values[k:k + 1, :], (128, 128)).T

    def fold(i):
        for k in range(ncol):
            csrc[i, k:k + 1, :] = jnp.sum(lane_a[k * 128:(k + 1) * 128, :].T, axis=0, keepdims=True)

    loads[0].wait()
    for b in range(rows // CHUNK):
        loads[b + 1].wait()
        tile[:, b * CHUNK:(b + 1) * CHUNK] = lax.dot_general(
            cen[...], pas[b * CHUNK:(b + 1) * CHUNK, :], (((1,), (1,)), ((), ())),
            preferred_element_type=F32,
        ) * (INV_TEMP * LOG2E)

    def col_first(r, carry):
        base = pl.ds(pl.multiple_of(r * 8, 8), 8)
        parts = [tile[base, c * 128:(c + 1) * 128] for c in range(nrow)]
        top = functools.reduce(jnp.maximum, parts)
        lane_a[base, :] = top
        lane_b[base, :] = functools.reduce(lax.add, [jnp.exp2(part - top) for part in parts])
        return carry

    lax.fori_loop(0, lists // 8, col_first, 0, unroll=2)
    for k in range(ncol):
        tops = lane_a[k * 128:(k + 1) * 128, :].T
        sums = lane_b[k * 128:(k + 1) * 128, :].T
        top = jnp.max(tops, axis=0, keepdims=True)
        total = jnp.sum(sums * jnp.exp2(tops - top), axis=0, keepdims=True)
        csrc[0, k:k + 1, :] = top + jnp.log(total) * LOG2E
    pl.semaphore_wait(barrier, 23)
    col_send(0)
    for b in range(rows // CHUNK):
        turned = pas[b * CHUNK:(b + 1) * CHUNK, :].T
        pas_t[:, :, b * CHUNK:(b + 1) * CHUNK] = turned.reshape(16, depth // 16, CHUNK)
    col_pot = share * LOG2E - lse2(col_recv(0))
    spread(col_pot)

    for b in range(rows // CHUNK):
        cols = [slice(b * CHUNK + c * 128, b * CHUNK + (c + 1) * 128) for c in range(CHUNK // 128)]

        def row_top(r, tops, cols=cols):
            base = pl.ds(pl.multiple_of(r * 8, 8), 8)
            add = lane_b[base, :]
            return tuple(jnp.maximum(top, tile[base, col] + add) for top, col in zip(tops, cols))

        tops = lax.fori_loop(
            0, lists // 8, row_top, tuple(jnp.full((8, 128), -jnp.inf, F32) for _ in cols), unroll=8
        )
        tops = [jnp.max(top, axis=0, keepdims=True) for top in tops]
        wide = [jnp.broadcast_to(top, (8, 128)) for top in tops]

        def row_exp(r, sums, cols=cols, wide=wide):
            base = pl.ds(pl.multiple_of(r * 8, 8), 8)
            add = lane_b[base, :]
            out = []
            for total, col, top in zip(sums, cols, wide):
                e = jnp.exp2(tile[base, col] + add - top)
                tile[base, col] = e
                out.append(total + e)
            return tuple(out)

        sums = lax.fori_loop(
            0, lists // 8, row_exp, tuple(jnp.zeros((8, 128), F32) for _ in cols), unroll=8
        )
        for c, (top, total) in enumerate(zip(tops, sums)):
            at = b * (CHUNK // 128) + c
            total = jnp.sum(total, axis=0, keepdims=True)
            m_ref[at:at + 1, :] = top
            rsrc[0, at:at + 1, :] = top + jnp.log(total) * LOG2E
    row_pot = -row_exchange(0, lse2)
    w_ref[...] = jnp.exp2(m_ref[...] + row_pot)
    u_ref[...] = w_ref[...]
    rp_ref[...] = row_pot * LN2
    cp_ref[...] = col_pot * LN2

    col_fac = row_fac = None
    for step in range(1, ITERS):
        us = [jnp.broadcast_to(u_ref[c:c + 1, :], (8, 128)) for c in range(nrow)]

        def col_sum(r, carry, us=us):
            base = pl.ds(pl.multiple_of(r * 8, 8), 8)
            lane_a[base, :] = tree_sum([tile[base, c * 128:(c + 1) * 128] * us[c] for c in range(nrow)])
            return carry

        lax.fori_loop(0, lists // 8, col_sum, 0, unroll=4)
        fold(step)
        col_send(step)
        col_fac = math.exp(share) / tree(col_recv(step), lax.add)
        spread(col_fac)
        for b in range(rows // CHUNK):
            cols = [slice(b * CHUNK + c * 128, b * CHUNK + (c + 1) * 128) for c in range(CHUNK // 128)]

            def row_sum(r, sums, cols=cols):
                base = pl.ds(pl.multiple_of(r * 8, 8), 8)
                fac = lane_b[base, :]
                return tuple(total + tile[base, col] * fac for total, col in zip(sums, cols))

            sums = lax.fori_loop(
                0, lists // 8, row_sum, tuple(jnp.zeros((8, 128), F32) for _ in cols), unroll=8
            )
            for c, total in enumerate(sums):
                at = b * (CHUNK // 128) + c
                rsrc[step, at:at + 1, :] = (
                    jnp.sum(total, axis=0, keepdims=True) * w_ref[at:at + 1, :]
                )
        row_fac = 1.0 / row_exchange(step, lambda values: tree(values, lax.add))
        u_ref[...] = w_ref[...] * row_fac
    rp_ref[...] += jnp.log(row_fac)
    cp_ref[...] += jnp.log(col_fac)

    us = [jnp.broadcast_to(u_ref[c:c + 1, :], (8, 128)) for c in range(nrow)]

    def plan(r, carry):
        base = pl.multiple_of(r * 16, 16)
        low, high = pl.ds(base, 8), pl.ds(base + 8, 8)
        first, second = [], []
        fac_low, fac_high = lane_b[low, :], lane_b[high, :]
        for c in range(nrow):
            col = slice(c * 128, (c + 1) * 128)
            a, b = tile[low, col] * us[c] * fac_low, tile[high, col] * us[c] * fac_high
            first.append(a)
            second.append(b)
            wts[pl.ds(base, 16), col] = jnp.concatenate([a, b], axis=0).astype(BF16)
        lane_a[low, :] = tree_sum(first)
        lane_a[high, :] = tree_sum(second)
        return carry

    lax.fori_loop(0, lists // 16, plan, 0)
    fold(ITERS)
    col_send(ITERS)

    half = depth // 32
    groups = lists // GROUP

    def hop(g, v, s):
        n = 8 >> s
        return pltpu.make_async_remote_copy(
            src_ref=stag.at[g, v, pl.ds(n, n)], dst_ref=rbs[s].at[g, v], send_sem=ss.at[s],
            recv_sem=sr.at[g, v, s], device_id=(flip(p, LINKS[ORDERS[v][s]]), l), device_id_type=MESH,
        )

    for g in range(groups):
        w = wts[g * GROUP:(g + 1) * GROUP, :]
        for q in range(4):
            left = jnp.concatenate([pas_t[flip(p, 4 * q + i)] for i in range(4)], axis=0)
            res = lax.dot_general(left, w, (((1,), (1,)), ((), ())), preferred_element_type=F32)
            for v in range(4):
                h, c = v // 2, v % 2
                for i in range(4):
                    stag[g, v, PLACES[v].index(4 * q + i)] = res[
                        i * 2 * half + h * half:i * 2 * half + (h + 1) * half, c * 128:(c + 1) * 128]
        for v in range(4):
            hop(g, v, 0).start()
    mass = None
    for s in range(1, 5):
        for g in range(groups):
            for v in range(4):
                hop(g, v, s - 1).wait_recv()
                n = 16 >> s
                if s < 4:
                    for i in list(range(n // 2, n)):
                        stag[g, v, i] += rbs[s - 1][g, v, i]
                    hop(g, v, s).start()
                    for i in range(n // 2):
                        stag[g, v, i] += rbs[s - 1][g, v, i]
                else:
                    if mass is None:
                        mass = tree(col_recv(ITERS), lax.add)
                    h, c = v // 2, v % 2
                    at = g * (GROUP // 128) + c
                    out_ref[h * half:(h + 1) * half, at * 128:(at + 1) * 128] = (
                        stag[g, v, 0] + rb3[g, v, 0]) / mass[at:at + 1, :]

    pltpu.make_async_copy(cslot, cslot, cs).wait()
    pltpu.make_async_copy(rpair, rpair, ps).wait()
    pltpu.make_async_copy(rslot, rslot, zs).wait()
    for s in range(4):
        pltpu.make_async_copy(rbs[s], rbs[s], ss.at[s]).wait()


def tree_sum(values):
    values = list(values)
    while len(values) > 1:
        pairs = [values[i] + values[i + 1] for i in range(0, len(values) - 1, 2)]
        values = pairs + values[len(values) - len(values) % 2:]
    return values[0]


def local(n_pass, n_list, passages, centroids):
    rows, depth = passages.shape
    lists = centroids.shape[0]
    nrow, ncol = rows // 128, lists // 128
    share = math.log(rows * n_pass / (lists * n_list))
    groups, part = lists // GROUP, depth // 32
    dma = pltpu.SemaphoreType.DMA
    vmem = pltpu.VMEM
    out, cp, rp = pl.pallas_call(
        functools.partial(kernel, share),
        out_shape=(
            jax.ShapeDtypeStruct((depth // n_pass, lists), F32),
            jax.ShapeDtypeStruct((ncol, 128), F32),
            jax.ShapeDtypeStruct((nrow, 128), F32),
        ),
        in_specs=[pl.BlockSpec(memory_space=pl.ANY)] * 2,
        out_specs=[pl.BlockSpec(memory_space=pltpu.VMEM)] * 3,
        scratch_shapes=[
            vmem((lists, depth), BF16),
            vmem((rows, depth), BF16),
            vmem((lists, rows), F32),
            vmem((16, depth // 16, rows), BF16),
            vmem((lists, rows), BF16),
            vmem((groups, 4, 16, part, 128), F32),
            vmem((groups, 4, 8, part, 128), F32),
            vmem((groups, 4, 4, part, 128), F32),
            vmem((groups, 4, 2, part, 128), F32),
            vmem((groups, 4, 1, part, 128), F32),
            vmem((lists, 128), F32),
            vmem((lists, 128), F32),
            vmem((ITERS + 1, ncol, 128), F32),
            vmem((ITERS + 1, 15, ncol, 128), F32),
            vmem((ITERS, nrow, 128), F32),
            vmem((ITERS, nrow, 128), F32),
            vmem((ITERS, nrow, 128), F32),
            vmem((ITERS, 7, nrow, 128), F32),
            vmem((nrow, 128), F32),
            vmem((nrow, 128), F32),
            vmem((nrow, 128), F32),
            dma((1 + rows // CHUNK,)),
            dma, dma((ITERS + 1,)),
            dma, dma((ITERS,)),
            dma, dma((ITERS,)),
            dma((4,)), dma((groups, 4, 4)),
        ],
        compiler_params=pltpu.CompilerParams(
            collective_id=0, has_side_effects=True, vmem_limit_bytes=56 << 20
        ),
        cost_estimate=pl.CostEstimate(
            flops=4 * rows * depth * lists, bytes_accessed=2 * (rows + lists) * depth,
            transcendentals=2 * rows * lists,
        ),
    )(passages, centroids)
    return out, cp.reshape(lists), rp.reshape(rows)


def solution(mesh):
    return jax.shard_map(
        functools.partial(local, mesh.shape["pass"], mesh.shape["list"]),
        mesh=mesh,
        in_specs=(P("pass", None), P("list", None)),
        out_specs=(P("pass", "list"), P("list"), P("pass")),
        check_vma=False,
    )
```

```python
import functools
import math

import jax
import jax.numpy as jnp
from jax import lax
from jax.experimental import pallas as pl
from jax.experimental.pallas import tpu as pltpu
from jax.sharding import PartitionSpec as P

ITERS = 4
INV_TEMP = 20.0
LOG2E = math.log2(math.e)
LN2 = math.log(2.0)
F32 = jnp.float32
BF16 = jnp.bfloat16
MESH = pl.DeviceIdType.MESH
CHUNK = 512
GROUP = 256
STEP = 4
NA = 16
LINKS = (4, 12, 1, 3)
ORDERS = ((0, 1, 2, 3), (1, 0, 3, 2), (2, 3, 0, 1), (3, 2, 1, 0))


def flip(index, bits):
    out = index
    b = 1
    while b <= bits:
        if bits & b:
            out = out + b * (1 - 2 * ((index // b) % 2))
        b *= 2
    return out


def place_of(order):
    first = order[0]
    axis_bits = lambda seq, unit: [0, unit * seq[1], unit * seq[0], unit * (seq[0] ^ seq[1])]
    low = {0: 1, 1: 3, 2: 1, 3: 3}
    unit = {0: 4, 1: 4, 2: 1, 3: 1}
    major = axis_bits((low[order[0]], low[order[1]]), unit[first])
    minor = axis_bits((low[order[2]], low[order[3]]), unit[order[2]])
    return [a + b for a in major for b in minor]


PLACES = [place_of(order) for order in ORDERS]


def tree(values, op):
    while len(values) > 1:
        values = [op(values[i], values[i + 1]) for i in range(0, len(values), 2)]
    return values[0]


def lse2(values):
    top = tree(values, jnp.maximum)
    total = tree([jnp.exp2(v - top) for v in values], lax.add)
    return top + jnp.log(total) * LOG2E


def ring_hops(bits, size):
    return max(min(abs((i ^ bits) - i), size - abs((i ^ bits) - i)) for i in range(size))


PASS_ORDER = sorted(range(1, 16), key=lambda k: -ring_hops(k // 4, 4) - ring_hops(k % 4, 4))
Z_ORDER = sorted(range(1, 8), key=lambda k: -ring_hops(k, 8))
LIST_ORDER = sorted(range(1, 16), key=lambda k: -ring_hops(k // 2, 8))


def kernel(
    share, na,
    pas_hbm, cen_hbm,
    out_ref, cp_ref, rp_ref,
    cen, pas, tile, gain, pas_t, wts, stag, rb0, rb1, rb2, rb3,
    lane_a, lane_b, lane_c, racc, csrc, cslot, asrc, apair, amid, aslot, bsrc, bslot,
    u_ref, w_ref, m_ref, cfac, in_sem, cs, cr, ps, pr, zs, zr, bs, br, ss, sr,
):
    rows, depth = pas.shape
    lists = cen.shape[0]
    nrow, ncol = rows // 128, lists // 128
    nhalf = ncol // 2
    p, l = lax.axis_index("pass"), lax.axis_index("list")
    rbs = (rb0, rb1, rb2, rb3)
    add = lambda values: tree(values, lax.add)

    loads = [pltpu.make_async_copy(cen_hbm, cen, in_sem.at[0])]
    for b in range(rows // CHUNK):
        part = pl.ds(b * CHUNK, CHUNK)
        loads.append(pltpu.make_async_copy(pas_hbm.at[part], pas.at[part], in_sem.at[b + 1]))
    for load in loads:
        load.start()

    barrier = pltpu.get_barrier_semaphore()
    for k in PASS_ORDER:
        pl.semaphore_signal(barrier, inc=1, device_id=(flip(p, k), l), device_id_type=MESH)
    for k in LIST_ORDER:
        pl.semaphore_signal(barrier, inc=1, device_id=(p, flip(l, k)), device_id_type=MESH)

    def col_send(i, h):
        for k in PASS_ORDER:
            pltpu.make_async_remote_copy(
                src_ref=csrc.at[i, h], dst_ref=cslot.at[i, h, k - 1], send_sem=cs,
                recv_sem=cr.at[i, h], device_id=(flip(p, k), l), device_id_type=MESH,
            ).start()

    def col_recv(i, h):
        pltpu.make_async_copy(cslot.at[i, h], cslot.at[i, h], cr.at[i, h]).wait()
        return [csrc[i, h]] + [cslot[i, h, k] for k in range(15)]

    def a_pair(i):
        return pltpu.make_async_remote_copy(
            src_ref=asrc.at[i], dst_ref=apair.at[i], send_sem=ps, recv_sem=pr.at[i],
            device_id=(p, flip(l, 1)), device_id_type=MESH,
        )

    def a_send(i, combine):
        a_pair(i).wait_recv()
        amid[i] = combine([asrc[i], apair[i]])
        for k in Z_ORDER:
            pltpu.make_async_remote_copy(
                src_ref=amid.at[i], dst_ref=aslot.at[i, k - 1], send_sem=zs, recv_sem=zr.at[i],
                device_id=(p, flip(l, 2 * k)), device_id_type=MESH,
            ).start()

    def a_recv(i, combine):
        pltpu.make_async_copy(aslot.at[i], aslot.at[i], zr.at[i]).wait()
        return combine([amid[i]] + [aslot[i, k] for k in range(7)])

    def b_send(i):
        for k in LIST_ORDER:
            pltpu.make_async_remote_copy(
                src_ref=bsrc.at[i], dst_ref=bslot.at[i, k - 1], send_sem=bs, recv_sem=br.at[i],
                device_id=(p, flip(l, k)), device_id_type=MESH,
            ).start()

    def b_recv(i, combine):
        pltpu.make_async_copy(bslot.at[i], bslot.at[i], br.at[i]).wait()
        return combine([bsrc[i]] + [bslot[i, k] for k in range(15)])

    def loop(first, last, body):
        def step(i, carry):
            body(i)
            return carry

        lax.fori_loop(first, last, step, 0)

    def unrolled(first, last, body):
        for i in range(first, last):
            body(i)

    def send_rows(i, combine, sweep):
        def part(ref, first):
            def body(b):
                for c, value in enumerate(sweep(b)):
                    ref[i, b * STEP + c - first:b * STEP + c - first + 1, :] = value

            return body

        unrolled(0, na // STEP, part(asrc, 0))
        a_pair(i).start()
        unrolled(na // STEP, nrow // STEP, part(bsrc, na))
        b_send(i)
        a_send(i, combine)

    part_a, part_b = slice(0, na), slice(na, nrow)

    def spread(values, h):
        for k in range(nhalf):
            at = pl.multiple_of((h * nhalf + k) * 128, 128)
            lane_b[pl.ds(at, 128), :] = jnp.broadcast_to(values[k:k + 1, :], (128, 128)).T

    def fold(i, h, ref):
        for k in range(nhalf):
            at = pl.multiple_of((h * nhalf + k) * 128, 128)
            csrc[i, h, k:k + 1, :] = jnp.sum(ref[pl.ds(at, 128), :].T, axis=0, keepdims=True)

    loads[0].wait()

    def logits(b):
        part = pl.ds(pl.multiple_of(b * CHUNK, CHUNK), CHUNK)
        pltpu.make_async_copy(pas_hbm.at[part], pas.at[part], in_sem.at[b + 1]).wait()
        tile[:, part] = lax.dot_general(
            cen[...], pas[part, :], (((1,), (1,)), ((), ())), preferred_element_type=F32
        ) * (INV_TEMP * LOG2E)

    loop(0, rows // CHUNK, logits)

    def col_first(h):
        def body(r, carry):
            base = pl.ds(pl.multiple_of(h * lists // 2 + r * 8, 8), 8)
            parts = [tile[base, c * 128:(c + 1) * 128] for c in range(nrow)]
            top = functools.reduce(jnp.maximum, parts)
            lane_a[base, :] = top
            lane_b[base, :] = functools.reduce(lax.add, [jnp.exp2(part - top) for part in parts])
            return carry

        lax.fori_loop(0, lists // 16, body, 0, unroll=2)
        for k in range(nhalf):
            at = pl.ds(pl.multiple_of((h * nhalf + k) * 128, 128), 128)
            tops = lane_a[at, :].T
            sums = lane_b[at, :].T
            top = jnp.max(tops, axis=0, keepdims=True)
            total = jnp.sum(sums * jnp.exp2(tops - top), axis=0, keepdims=True)
            csrc[0, h, k:k + 1, :] = top + jnp.log(total) * LOG2E
        col_send(0, h)

    pl.semaphore_wait(barrier, 30)
    loop(0, 2, col_first)

    def turn(b):
        part = pl.ds(pl.multiple_of(b * CHUNK, CHUNK), CHUNK)
        pas_t[:, :, part] = pas[part, :].T.reshape(16, depth // 16, CHUNK)

    loop(0, rows // CHUNK, turn)
    for h in range(2):
        col_pot = share * LOG2E - lse2(col_recv(0, h))
        cp_ref[h * nhalf:(h + 1) * nhalf, :] = col_pot * LN2
        spread(col_pot, h)

    def columns(b):
        return [slice((b * STEP + c) * 128, (b * STEP + c + 1) * 128) for c in range(STEP)]

    def row_first(b):
        cols = columns(b)

        def row_top(r, tops):
            out = []
            for j in range(2):
                base = pl.ds(pl.multiple_of(r * 16, 16) + 8 * j, 8)
                pot = lane_b[base, :]
                out += [jnp.maximum(top, tile[base, col] + pot)
                        for top, col in zip(tops[j * STEP:(j + 1) * STEP], cols)]
            return tuple(out)

        tops = lax.fori_loop(
            0, lists // 16, row_top,
            tuple(jnp.full((8, 128), -jnp.inf, F32) for _ in range(2 * STEP)), unroll=4,
        )
        tops = [jnp.max(jnp.maximum(tops[c], tops[c + STEP]), axis=0, keepdims=True) for c in range(STEP)]
        wide = [jnp.broadcast_to(top, (8, 128)) for top in tops]

        def row_exp(r, sums):
            out = []
            for j in range(2):
                base = pl.ds(pl.multiple_of(r * 16, 16) + 8 * j, 8)
                pot = lane_b[base, :]
                for total, col, top in zip(sums[j * STEP:(j + 1) * STEP], cols, wide):
                    e = jnp.exp2(tile[base, col] + pot - top)
                    gain[base, col] = e
                    out.append(total + e)
            return tuple(out)

        sums = lax.fori_loop(
            0, lists // 16, row_exp, tuple(jnp.zeros((8, 128), F32) for _ in range(2 * STEP)), unroll=4
        )
        result = []
        for c, top in enumerate(tops):
            total = jnp.sum(sums[c] + sums[c + STEP], axis=0, keepdims=True)
            m_ref[pl.ds(b * STEP + c, 1), :] = top
            result.append(top + jnp.log(total) * LOG2E)
        return result

    send_rows(0, lse2, row_first)

    def first_factors(part, row_pot):
        rp_ref[part, :] = row_pot * LN2
        w_ref[part, :] = jnp.exp2(m_ref[part, :] + row_pot)
        u_ref[part, :] = w_ref[part, :]

    def next_factors(part, row_fac):
        u_ref[part, :] = w_ref[part, :] * row_fac
        m_ref[part, :] = row_fac

    def factors(part):
        return [jnp.broadcast_to(u_ref[c:c + 1, :], (8, 128)) for c in range(part.start, part.stop)]

    def col_sweep(part, first, count, out, start):
        us = factors(part)

        def body(r, carry):
            base = pl.ds(pl.multiple_of(first + r * 8, 8), 8)
            total = tree_sum([gain[base, c * 128:(c + 1) * 128] * us[c - part.start]
                              for c in range(part.start, part.stop)])
            out[base, :] = total if start is None else total + start[base, :]
            return carry

        lax.fori_loop(0, count // 8, body, 0, unroll=4)

    def row_sweep(b, h):
        cols = columns(b)

        def body(r, sums):
            out = []
            for j in range(2):
                base = pl.ds(pl.multiple_of(h * lists // 2 + r * 16, 16) + 8 * j, 8)
                fac = lane_b[base, :]
                out += [total + gain[base, col] * fac
                        for total, col in zip(sums[j * STEP:(j + 1) * STEP], cols)]
            return tuple(out)

        sums = lax.fori_loop(
            0, lists // 32, body, tuple(jnp.zeros((8, 128), F32) for _ in range(2 * STEP)), unroll=4
        )
        return [sums[c] + sums[c + STEP] for c in range(STEP)], cols

    def plan(part, first, count, out, start):
        us = factors(part)

        def body(r):
            base = pl.multiple_of(first + r * 16, 16)
            low, high = pl.ds(base, 8), pl.ds(base + 8, 8)
            fac_low, fac_high = lane_b[low, :], lane_b[high, :]
            sums_low, sums_high = [], []
            for c in range(part.start, part.stop):
                col = slice(c * 128, (c + 1) * 128)
                a = gain[low, col] * us[c - part.start] * fac_low
                b = gain[high, col] * us[c - part.start] * fac_high
                sums_low.append(a)
                sums_high.append(b)
                wts[pl.ds(base, 16), col] = jnp.concatenate([a, b], axis=0).astype(BF16)
            sum_low, sum_high = tree_sum(sums_low), tree_sum(sums_high)
            out[low, :] = sum_low if start is None else sum_low + start[low, :]
            out[high, :] = sum_high if start is None else sum_high + start[high, :]

        loop(0, count // 16, body)

    first_factors(part_b, -b_recv(0, lse2))
    col_sweep(part_b, 0, lists, lane_a, None)
    first_factors(part_a, -a_recv(0, lse2))

    def iteration(step):
        def col_half(h):
            col_sweep(part_a, h * lists // 2, lists // 2, lane_c, lane_a)
            fold(step, h, lane_c)
            col_send(step, h)

        loop(0, 2, col_half)
        for h in range(2):
            col_fac = math.exp(share) / add(col_recv(step, h))
            cfac[h] = col_fac
            spread(col_fac, h)
            if h == 0:
                def first_half(b):
                    sums, cols = row_sweep(b, 0)
                    for total, col in zip(sums, cols):
                        racc[:, col] = total

                unrolled(0, nrow // STEP, first_half)

        def last_half(b):
            sums, cols = row_sweep(b, 1)
            return [
                jnp.sum(total + racc[:, col], axis=0, keepdims=True) * w_ref[pl.ds(b * STEP + c, 1), :]
                for c, (total, col) in enumerate(zip(sums, cols))
            ]

        send_rows(step, add, last_half)
        next_factors(part_b, 1.0 / b_recv(step, add))

        @pl.when(step < ITERS - 1)
        def _():
            col_sweep(part_b, 0, lists, lane_a, None)

        @pl.when(step == ITERS - 1)
        def _():
            plan(part_b, 0, lists, lane_a, None)

        next_factors(part_a, 1.0 / a_recv(step, add))

    loop(1, ITERS, iteration)

    half = depth // 32
    groups = lists // GROUP

    def hop(g, v, s):
        n = 8 >> s
        return pltpu.make_async_remote_copy(
            src_ref=stag.at[g, v, pl.ds(n, n)], dst_ref=rbs[s].at[g, v], send_sem=ss.at[s],
            recv_sem=sr.at[g, v, s], device_id=(flip(p, LINKS[ORDERS[v][s]]), l), device_id_type=MESH,
        )

    def group_sums(g):
        first = pl.multiple_of(g * GROUP, GROUP)
        plan(part_a, first, GROUP, lane_c, lane_a)
        w = wts[pl.ds(first, GROUP), :]
        left = jnp.concatenate([pas_t[flip(p, i)] for i in range(16)], axis=0)
        res = lax.dot_general(left, w, (((1,), (1,)), ((), ())), preferred_element_type=F32)
        for v in range(4):
            h, c = v // 2, v % 2
            for i in range(16):
                stag[g, v, PLACES[v].index(i)] = res[
                    (2 * i + h) * half:(2 * i + h + 1) * half, c * 128:(c + 1) * 128]
        for v in range(4):
            hop(g, v, 0).start()

    loop(0, groups, group_sums)

    def mass_half(h):
        fold(ITERS, h, lane_c)
        col_send(ITERS, h)

    loop(0, 2, mass_half)
    rp_ref[...] += jnp.log(m_ref[...])
    for h in range(2):
        cp_ref[h * nhalf:(h + 1) * nhalf, :] += jnp.log(cfac[h])
    for s in range(1, 4):
        def reduce(g, s=s):
            n = 16 >> s
            for v in range(4):
                hop(g, v, s - 1).wait_recv()
                for i in range(n // 2, n):
                    stag[g, v, i] += rbs[s - 1][g, v, i]
                hop(g, v, s).start()
                for i in range(n // 2):
                    stag[g, v, i] += rbs[s - 1][g, v, i]

        loop(0, groups, reduce)
    mass = [add(col_recv(ITERS, h)) for h in range(2)]
    for g in range(groups):
        for v in range(4):
            hop(g, v, 3).wait_recv()
            h, c = v // 2, v % 2
            at = g * (GROUP // 128) + c
            out_ref[h * half:(h + 1) * half, at * 128:(at + 1) * 128] = (
                stag[g, v, 0] + rb3[g, v, 0]) / mass[at // nhalf][at % nhalf:at % nhalf + 1, :]

    for ref, sem in ((cslot, cs), (apair, ps), (aslot, zs), (bslot, bs)):
        pltpu.make_async_copy(ref, ref, sem).wait()
    for s in range(4):
        pltpu.make_async_copy(rbs[s], rbs[s], ss.at[s]).wait()


def copy_out(*refs):
    n = len(refs) // 2
    for src, dst in zip(refs[:n], refs[n:]):
        dst[...] = src[...]


def tree_sum(values):
    values = list(values)
    while len(values) > 1:
        pairs = [values[i] + values[i + 1] for i in range(0, len(values) - 1, 2)]
        values = pairs + values[len(values) - len(values) % 2:]
    return values[0]


def local(n_pass, n_list, passages, centroids):
    rows, depth = passages.shape
    lists = centroids.shape[0]
    nrow, ncol = rows // 128, lists // 128
    na = NA
    share = math.log(rows * n_pass / (lists * n_list))
    groups, part = lists // GROUP, depth // 32
    dma = pltpu.SemaphoreType.DMA
    vmem = pltpu.VMEM
    shapes = (
        jax.ShapeDtypeStruct((depth // n_pass, lists), F32),
        jax.ShapeDtypeStruct((ncol, 128), F32),
        jax.ShapeDtypeStruct((nrow, 128), F32),
    )
    whole = pl.BlockSpec(memory_space=pltpu.VMEM)
    results = pl.pallas_call(
        functools.partial(kernel, share, na),
        out_shape=shapes,
        in_specs=[pl.BlockSpec(memory_space=pl.ANY)] * 2,
        out_specs=[whole] * 3,
        scratch_shapes=[
            vmem((lists, depth), BF16),
            vmem((rows, depth), BF16),
            vmem((lists, rows), F32),
            vmem((lists, rows), F32),
            vmem((16, depth // 16, rows), BF16),
            vmem((lists, rows), BF16),
            vmem((groups, 4, 16, part, 128), F32),
            vmem((groups, 4, 8, part, 128), F32),
            vmem((groups, 4, 4, part, 128), F32),
            vmem((groups, 4, 2, part, 128), F32),
            vmem((groups, 4, 1, part, 128), F32),
            vmem((lists, 128), F32),
            vmem((lists, 128), F32),
            vmem((lists, 128), F32),
            vmem((8, rows), F32),
            vmem((ITERS + 1, 2, ncol // 2, 128), F32),
            vmem((ITERS + 1, 2, 15, ncol // 2, 128), F32),
            vmem((ITERS, na, 128), F32),
            vmem((ITERS, na, 128), F32),
            vmem((ITERS, na, 128), F32),
            vmem((ITERS, 7, na, 128), F32),
            vmem((ITERS, nrow - na, 128), F32),
            vmem((ITERS, 15, nrow - na, 128), F32),
            vmem((nrow, 128), F32),
            vmem((nrow, 128), F32),
            vmem((nrow, 128), F32),
            vmem((2, ncol // 2, 128), F32),
            dma((1 + rows // CHUNK,)),
            dma, dma((ITERS + 1, 2)),
            dma, dma((ITERS,)),
            dma, dma((ITERS,)),
            dma, dma((ITERS,)),
            dma((4,)), dma((groups, 4, 4)),
        ],
        compiler_params=pltpu.CompilerParams(
            collective_id=0, has_side_effects=True, vmem_limit_bytes=56 << 20
        ),
        cost_estimate=pl.CostEstimate(
            flops=4 * rows * depth * lists, bytes_accessed=2 * (rows + lists) * depth,
            transcendentals=2 * rows * lists,
        ),
    )(passages, centroids)
    out, cp, rp = pl.pallas_call(
        copy_out, out_shape=shapes, in_specs=[whole] * 3, out_specs=[whole] * 3
    )(*results)
    return out, cp.reshape(lists), rp.reshape(rows)


def solution(mesh):
    return jax.shard_map(
        functools.partial(local, mesh.shape["pass"], mesh.shape["list"]),
        mesh=mesh,
        in_specs=(P("pass", None), P("list", None)),
        out_specs=(P("pass", "list"), P("list"), P("pass")),
        check_vma=False,
    )
```

```python
import functools
import math

import jax
import jax.numpy as jnp
from jax import lax
from jax.experimental import pallas as pl
from jax.experimental.pallas import tpu as pltpu
from jax.sharding import PartitionSpec as P

ITERS = 4
INV_TEMP = 20.0
LOG2E = math.log2(math.e)
LN2 = math.log(2.0)
F32 = jnp.float32
BF16 = jnp.bfloat16
MESH = pl.DeviceIdType.MESH
CHUNK = 512
GROUP = 256
STEP = 4
NA = 16
PARTS = 1
LAST_ORDER = (3, 2, 1)
LINKS = (4, 12, 1, 3)
ORDERS = ((0, 1, 2, 3), (1, 0, 3, 2), (2, 3, 0, 1), (3, 2, 1, 0))


def flip(index, bits):
    out = index
    b = 1
    while b <= bits:
        if bits & b:
            out = out + b * (1 - 2 * ((index // b) % 2))
        b *= 2
    return out


def place_of(order):
    first = order[0]
    axis_bits = lambda seq, unit: [0, unit * seq[1], unit * seq[0], unit * (seq[0] ^ seq[1])]
    low = {0: 1, 1: 3, 2: 1, 3: 3}
    unit = {0: 4, 1: 4, 2: 1, 3: 1}
    major = axis_bits((low[order[0]], low[order[1]]), unit[first])
    minor = axis_bits((low[order[2]], low[order[3]]), unit[order[2]])
    return [a + b for a in major for b in minor]


PLACES = [place_of(order) for order in ORDERS]


def chains(values, op, count=4):
    heads = list(values[:count])
    for i, value in enumerate(values[count:]):
        heads[i % count] = op(heads[i % count], value)
    return tree(heads, op)


def tree(values, op):
    while len(values) > 1:
        values = [op(values[i], values[i + 1]) for i in range(0, len(values), 2)]
    return values[0]


def lse2(values):
    top = tree(values, jnp.maximum)
    total = tree([jnp.exp2(v - top) for v in values], lax.add)
    return top + jnp.log(total) * LOG2E


def ring_hops(bits, size):
    return max(min(abs((i ^ bits) - i), size - abs((i ^ bits) - i)) for i in range(size))


PASS_ORDER = sorted(range(1, 16), key=lambda k: -ring_hops(k // 4, 4) - ring_hops(k % 4, 4))
Z_ORDER = sorted(range(1, 8), key=lambda k: -ring_hops(k, 8))
LIST_ORDER = sorted(range(1, 16), key=lambda k: -ring_hops(k // 2, 8))


def kernel(
    share, na,
    pas_hbm, cen_hbm,
    out_ref, cp_ref, rp_ref,
    cen, pas, tile, gain, pas_t, wts, stag, rb0, rb1, rb2,
    lane_a, lane_b, lane_c, racc, csrc, cslot, asrc, apair, amid, aslot, bsrc, bslot,
    u_ref, w_ref, m_ref, cfac, in_sem, cs, cr, ps, pr, zs, zr, bs, br, ss, sr,
):
    rows, depth = pas.shape
    lists = cen.shape[0]
    nrow, ncol = rows // 128, lists // 128
    nhalf = ncol // PARTS
    p, l = lax.axis_index("pass"), lax.axis_index("list")
    add = lambda values: tree(values, lax.add)

    loads = [pltpu.make_async_copy(cen_hbm, cen, in_sem.at[0])]
    for b in range(rows // CHUNK):
        part = pl.ds(b * CHUNK, CHUNK)
        loads.append(pltpu.make_async_copy(pas_hbm.at[part], pas.at[part], in_sem.at[b + 1]))
    for load in loads:
        load.start()

    barrier = pltpu.get_barrier_semaphore()
    for k in PASS_ORDER:
        pl.semaphore_signal(barrier, inc=1, device_id=(flip(p, k), l), device_id_type=MESH)
    for k in LIST_ORDER:
        pl.semaphore_signal(barrier, inc=1, device_id=(p, flip(l, k)), device_id_type=MESH)

    def col_send(i, h):
        for k in PASS_ORDER:
            pltpu.make_async_remote_copy(
                src_ref=csrc.at[i, h], dst_ref=cslot.at[i, h, k - 1], send_sem=cs,
                recv_sem=cr.at[i, h], device_id=(flip(p, k), l), device_id_type=MESH,
            ).start()

    def col_recv(i, h):
        pltpu.make_async_copy(cslot.at[i, h], cslot.at[i, h], cr.at[i, h]).wait()
        return [csrc[i, h]] + [cslot[i, h, k] for k in range(15)]

    def a_pair(i):
        return pltpu.make_async_remote_copy(
            src_ref=asrc.at[i], dst_ref=apair.at[i], send_sem=ps, recv_sem=pr.at[i],
            device_id=(p, flip(l, 1)), device_id_type=MESH,
        )

    def a_send(i, combine):
        a_pair(i).wait_recv()
        amid[i] = combine([asrc[i], apair[i]])
        for k in Z_ORDER:
            pltpu.make_async_remote_copy(
                src_ref=amid.at[i], dst_ref=aslot.at[i, k - 1], send_sem=zs, recv_sem=zr.at[i],
                device_id=(p, flip(l, 2 * k)), device_id_type=MESH,
            ).start()

    def a_recv(i, combine):
        pltpu.make_async_copy(aslot.at[i], aslot.at[i], zr.at[i]).wait()
        return combine([amid[i]] + [aslot[i, k] for k in range(7)])

    def b_send(i):
        for k in LIST_ORDER:
            pltpu.make_async_remote_copy(
                src_ref=bsrc.at[i], dst_ref=bslot.at[i, k - 1], send_sem=bs, recv_sem=br.at[i],
                device_id=(p, flip(l, k)), device_id_type=MESH,
            ).start()

    def b_recv(i, combine):
        pltpu.make_async_copy(bslot.at[i], bslot.at[i], br.at[i]).wait()
        return combine([bsrc[i]] + [bslot[i, k] for k in range(15)])

    def loop(first, last, body):
        def step(i, carry):
            body(i)
            return carry

        lax.fori_loop(first, last, step, 0)

    def unrolled(first, last, body):
        for i in range(first, last):
            body(i)

    def send_rows(i, combine, sweep):
        def part(ref, first):
            def body(b):
                for c, value in enumerate(sweep(b)):
                    ref[i, b * STEP + c - first:b * STEP + c - first + 1, :] = value

            return body

        unrolled(0, na // STEP, part(asrc, 0))
        a_pair(i).start()
        unrolled(na // STEP, nrow // STEP, part(bsrc, na))
        b_send(i)
        a_send(i, combine)

    part_a, part_b = slice(0, na), slice(na, nrow)

    def spread(values, h):
        for k in range(nhalf):
            at = pl.multiple_of((h * nhalf + k) * 128, 128)
            lane_b[pl.ds(at, 128), :] = jnp.broadcast_to(values[k:k + 1, :], (128, 128)).T

    def fold(i, h, ref):
        for k in range(nhalf):
            at = pl.multiple_of((h * nhalf + k) * 128, 128)
            csrc[i, h, k:k + 1, :] = jnp.sum(ref[pl.ds(at, 128), :].T, axis=0, keepdims=True)

    loads[0].wait()

    def logits(b):
        part = pl.ds(pl.multiple_of(b * CHUNK, CHUNK), CHUNK)
        pltpu.make_async_copy(pas_hbm.at[part], pas.at[part], in_sem.at[b + 1]).wait()
        tile[:, part] = lax.dot_general(
            cen[...], pas[part, :], (((1,), (1,)), ((), ())), preferred_element_type=F32
        ) * (INV_TEMP * LOG2E)

    loop(0, rows // CHUNK, logits)

    def col_first(h):
        def body(r, carry):
            base = pl.ds(pl.multiple_of(h * (lists // PARTS) + r * 8, 8), 8)
            parts = [tile[base, c * 128:(c + 1) * 128] for c in range(nrow)]
            top = chains(parts, jnp.maximum)
            lane_a[base, :] = top
            lane_b[base, :] = chains([jnp.exp2(part - top) for part in parts], lax.add)
            return carry

        lax.fori_loop(0, lists // (8 * PARTS), body, 0, unroll=4)
        for k in range(nhalf):
            at = pl.ds(pl.multiple_of((h * nhalf + k) * 128, 128), 128)
            tops = lane_a[at, :].T
            sums = lane_b[at, :].T
            top = jnp.max(tops, axis=0, keepdims=True)
            total = jnp.sum(sums * jnp.exp2(tops - top), axis=0, keepdims=True)
            csrc[0, h, k:k + 1, :] = top + jnp.log(total) * LOG2E
        col_send(0, h)

    pl.semaphore_wait(barrier, 30)
    loop(0, PARTS, col_first)

    def turn(b):
        part = pl.ds(pl.multiple_of(b * CHUNK, CHUNK), CHUNK)
        pas_t[:, :, part] = pas[part, :].T.reshape(16, depth // 16, CHUNK)

    loop(0, rows // CHUNK, turn)
    for h in range(PARTS):
        col_pot = share * LOG2E - lse2(col_recv(0, h))
        cp_ref[h * nhalf:(h + 1) * nhalf, :] = col_pot * LN2
        spread(col_pot, h)

    def columns(b):
        return [slice((b * STEP + c) * 128, (b * STEP + c + 1) * 128) for c in range(STEP)]

    def row_first(b):
        cols = columns(b)

        def row_top(r, tops):
            out = []
            for j in range(2):
                base = pl.ds(pl.multiple_of(r * 16, 16) + 8 * j, 8)
                pot = lane_b[base, :]
                out += [jnp.maximum(top, tile[base, col] + pot)
                        for top, col in zip(tops[j * STEP:(j + 1) * STEP], cols)]
            return tuple(out)

        tops = lax.fori_loop(
            0, lists // 16, row_top,
            tuple(jnp.full((8, 128), -jnp.inf, F32) for _ in range(2 * STEP)), unroll=4,
        )
        tops = [jnp.max(jnp.maximum(tops[c], tops[c + STEP]), axis=0, keepdims=True) for c in range(STEP)]
        wide = [jnp.broadcast_to(top, (8, 128)) for top in tops]

        def row_exp(r, sums):
            out = []
            for j in range(2):
                base = pl.ds(pl.multiple_of(r * 16, 16) + 8 * j, 8)
                pot = lane_b[base, :]
                for total, col, top in zip(sums[j * STEP:(j + 1) * STEP], cols, wide):
                    e = jnp.exp2(tile[base, col] + pot - top)
                    gain[base, col] = e
                    out.append(total + e)
            return tuple(out)

        sums = lax.fori_loop(
            0, lists // 16, row_exp, tuple(jnp.zeros((8, 128), F32) for _ in range(2 * STEP)), unroll=4
        )
        result = []
        for c, top in enumerate(tops):
            total = jnp.sum(sums[c] + sums[c + STEP], axis=0, keepdims=True)
            m_ref[pl.ds(b * STEP + c, 1), :] = top
            result.append(top + jnp.log(total) * LOG2E)
        return result

    send_rows(0, lse2, row_first)

    def first_factors(part, row_pot):
        rp_ref[part, :] = row_pot * LN2
        w_ref[part, :] = jnp.exp2(m_ref[part, :] + row_pot)
        u_ref[part, :] = w_ref[part, :]

    def next_factors(part, row_fac):
        u_ref[part, :] = w_ref[part, :] * row_fac
        m_ref[part, :] = row_fac

    def factors(part):
        return [jnp.broadcast_to(u_ref[c:c + 1, :], (8, 128)) for c in range(part.start, part.stop)]

    def col_sweep(part, first, count, out, start):
        us = factors(part)

        def body(r, carry):
            base = pl.ds(pl.multiple_of(first + r * 8, 8), 8)
            total = tree_sum([gain[base, c * 128:(c + 1) * 128] * us[c - part.start]
                              for c in range(part.start, part.stop)])
            out[base, :] = total if start is None else total + start[base, :]
            return carry

        lax.fori_loop(0, count // 8, body, 0, unroll=4)

    def row_sweep(b, h):
        cols = columns(b)

        def body(r, sums):
            out = []
            for j in range(2):
                base = pl.ds(pl.multiple_of(h * (lists // PARTS) + r * 16, 16) + 8 * j, 8)
                fac = lane_b[base, :]
                out += [total + gain[base, col] * fac
                        for total, col in zip(sums[j * STEP:(j + 1) * STEP], cols)]
            return tuple(out)

        sums = lax.fori_loop(
            0, lists // (16 * PARTS), body, tuple(jnp.zeros((8, 128), F32) for _ in range(2 * STEP)), unroll=4
        )
        return [sums[c] + sums[c + STEP] for c in range(STEP)], cols

    def plan(part, first, count, out, start):
        us = factors(part)

        def body(r):
            base = pl.multiple_of(first + r * 16, 16)
            low, high = pl.ds(base, 8), pl.ds(base + 8, 8)
            fac_low, fac_high = lane_b[low, :], lane_b[high, :]
            sums_low, sums_high = [], []
            for c in range(part.start, part.stop):
                col = slice(c * 128, (c + 1) * 128)
                a = gain[low, col] * us[c - part.start] * fac_low
                b = gain[high, col] * us[c - part.start] * fac_high
                sums_low.append(a)
                sums_high.append(b)
                wts[pl.ds(base, 16), col] = jnp.concatenate([a, b], axis=0).astype(BF16)
            sum_low, sum_high = tree_sum(sums_low), tree_sum(sums_high)
            out[low, :] = sum_low if start is None else sum_low + start[low, :]
            out[high, :] = sum_high if start is None else sum_high + start[high, :]

        loop(0, count // 16, body)

    first_factors(part_b, -b_recv(0, lse2))
    col_sweep(part_b, 0, lists, lane_a, None)
    first_factors(part_a, -a_recv(0, lse2))

    def iteration(step):
        def col_half(h):
            col_sweep(part_a, h * (lists // PARTS), lists // PARTS, lane_c, lane_a)
            fold(step, h, lane_c)
            col_send(step, h)

        loop(0, PARTS, col_half)
        for h in range(PARTS):
            col_fac = math.exp(share) / add(col_recv(step, h))
            cfac[h] = col_fac
            spread(col_fac, h)
            if h < PARTS - 1:
                def first_half(b):
                    sums, cols = row_sweep(b, 0)
                    for total, col in zip(sums, cols):
                        racc[:, col] = total

                unrolled(0, nrow // STEP, first_half)

        def last_half(b):
            sums, cols = row_sweep(b, PARTS - 1)
            return [
                jnp.sum(total + racc[:, col] if PARTS > 1 else total, axis=0, keepdims=True) * w_ref[pl.ds(b * STEP + c, 1), :]
                for c, (total, col) in enumerate(zip(sums, cols))
            ]

        send_rows(step, add, last_half)
        next_factors(part_b, 1.0 / b_recv(step, add))

        @pl.when(step < ITERS - 1)
        def _():
            col_sweep(part_b, 0, lists, lane_a, None)

        @pl.when(step == ITERS - 1)
        def _():
            plan(part_b, 0, lists, lane_a, None)

        next_factors(part_a, 1.0 / a_recv(step, add))

    loop(1, ITERS, iteration)

    half = depth // 32
    groups = lists // GROUP

    def hop(g, v, s):
        n = 8 >> s
        return pltpu.make_async_remote_copy(
            src_ref=stag.at[g, v, pl.ds(n, n)], dst_ref=(rb0, rb1)[s].at[g, v], send_sem=ss.at[s],
            recv_sem=sr.at[g, v, s], device_id=(flip(p, LINKS[ORDERS[v][s]]), l), device_id_type=MESH,
        )

    def group_sums(g):
        first = pl.multiple_of(g * GROUP, GROUP)
        plan(part_a, first, GROUP, lane_c, lane_a)
        w = wts[pl.ds(first, GROUP), :]
        left = jnp.concatenate([pas_t[flip(p, i)] for i in range(16)], axis=0)
        res = lax.dot_general(left, w, (((1,), (1,)), ((), ())), preferred_element_type=F32)
        for v in range(4):
            h, c = v // 2, v % 2
            for i in range(16):
                stag[g, v, PLACES[v].index(i)] = res[
                    (2 * i + h) * half:(2 * i + h + 1) * half, c * 128:(c + 1) * 128]
        for v in range(4):
            hop(g, v, 0).start()

    loop(0, groups, group_sums)

    def mass_half(h):
        fold(ITERS, h, lane_c)
        col_send(ITERS, h)

    loop(0, PARTS, mass_half)
    rp_ref[...] += jnp.log(m_ref[...])
    for h in range(PARTS):
        cp_ref[h * nhalf:(h + 1) * nhalf, :] += jnp.log(cfac[h])
    def second(g):
        for v in range(4):
            hop(g, v, 0).wait_recv()
            for i in range(4, 8):
                stag[g, v, i] += rb0[g, v, i]
            hop(g, v, 1).start()
            for i in range(4):
                stag[g, v, i] += rb0[g, v, i]

    def third(g):
        for v in range(4):
            hop(g, v, 1).wait_recv()
            for i in LAST_ORDER:
                stag[g, v, i] += rb1[g, v, i]
                pltpu.make_async_remote_copy(
                    src_ref=stag.at[g, v, i], dst_ref=rb2.at[g, v, i - 1], send_sem=ss.at[2],
                    recv_sem=sr.at[g, v, 2], device_id=(flip(p, PLACES[v][i]), l), device_id_type=MESH,
                ).start()
            stag[g, v, 0] += rb1[g, v, 0]

    loop(0, groups, second)
    loop(0, groups, third)
    mass = [add(col_recv(ITERS, h)) for h in range(PARTS)]
    for g in range(groups):
        for v in range(4):
            pltpu.make_async_copy(rb2.at[g, v], rb2.at[g, v], sr.at[g, v, 2]).wait()
            h, c = v // 2, v % 2
            at = g * (GROUP // 128) + c
            total = (stag[g, v, 0] + rb2[g, v, 0]) + (rb2[g, v, 1] + rb2[g, v, 2])
            out_ref[h * half:(h + 1) * half, at * 128:(at + 1) * 128] = (
                total / mass[at // nhalf][at % nhalf:at % nhalf + 1, :])

    for ref, sem in ((cslot, cs), (apair, ps), (aslot, zs), (bslot, bs)):
        pltpu.make_async_copy(ref, ref, sem).wait()
    for s, ref in enumerate((rb0, rb1, rb2)):
        pltpu.make_async_copy(ref, ref, ss.at[s]).wait()


def copy_out(*refs):
    n = len(refs) // 2
    for src, dst in zip(refs[:n], refs[n:]):
        dst[...] = src[...]


def tree_sum(values):
    values = list(values)
    while len(values) > 1:
        pairs = [values[i] + values[i + 1] for i in range(0, len(values) - 1, 2)]
        values = pairs + values[len(values) - len(values) % 2:]
    return values[0]


def local(n_pass, n_list, passages, centroids):
    rows, depth = passages.shape
    lists = centroids.shape[0]
    nrow, ncol = rows // 128, lists // 128
    na = NA
    share = math.log(rows * n_pass / (lists * n_list))
    groups, part = lists // GROUP, depth // 32
    dma = pltpu.SemaphoreType.DMA
    vmem = pltpu.VMEM
    shapes = (
        jax.ShapeDtypeStruct((depth // n_pass, lists), F32),
        jax.ShapeDtypeStruct((ncol, 128), F32),
        jax.ShapeDtypeStruct((nrow, 128), F32),
    )
    whole = pl.BlockSpec(memory_space=pltpu.VMEM)
    results = pl.pallas_call(
        functools.partial(kernel, share, na),
        out_shape=shapes,
        in_specs=[pl.BlockSpec(memory_space=pl.ANY)] * 2,
        out_specs=[whole] * 3,
        scratch_shapes=[
            vmem((lists, depth), BF16),
            vmem((rows, depth), BF16),
            vmem((lists, rows), F32),
            vmem((lists, rows), F32),
            vmem((16, depth // 16, rows), BF16),
            vmem((lists, rows), BF16),
            vmem((groups, 4, 16, part, 128), F32),
            vmem((groups, 4, 8, part, 128), F32),
            vmem((groups, 4, 4, part, 128), F32),
            vmem((groups, 4, 3, part, 128), F32),
            vmem((lists, 128), F32),
            vmem((lists, 128), F32),
            vmem((lists, 128), F32),
            vmem((8, rows), F32),
            vmem((ITERS + 1, PARTS, ncol // PARTS, 128), F32),
            vmem((ITERS + 1, PARTS, 15, ncol // PARTS, 128), F32),
            vmem((ITERS, na, 128), F32),
            vmem((ITERS, na, 128), F32),
            vmem((ITERS, na, 128), F32),
            vmem((ITERS, 7, na, 128), F32),
            vmem((ITERS, nrow - na, 128), F32),
            vmem((ITERS, 15, nrow - na, 128), F32),
            vmem((nrow, 128), F32),
            vmem((nrow, 128), F32),
            vmem((nrow, 128), F32),
            vmem((PARTS, ncol // PARTS, 128), F32),
            dma((1 + rows // CHUNK,)),
            dma, dma((ITERS + 1, PARTS)),
            dma, dma((ITERS,)),
            dma, dma((ITERS,)),
            dma, dma((ITERS,)),
            dma((3,)), dma((groups, 4, 3)),
        ],
        compiler_params=pltpu.CompilerParams(
            collective_id=0, has_side_effects=True, vmem_limit_bytes=56 << 20
        ),
        cost_estimate=pl.CostEstimate(
            flops=4 * rows * depth * lists, bytes_accessed=2 * (rows + lists) * depth,
            transcendentals=2 * rows * lists,
        ),
    )(passages, centroids)
    out, cp, rp = pl.pallas_call(
        copy_out, out_shape=shapes, in_specs=[whole] * 3, out_specs=[whole] * 3
    )(*results)
    return out, cp.reshape(lists), rp.reshape(rows)


def solution(mesh):
    return jax.shard_map(
        functools.partial(local, mesh.shape["pass"], mesh.shape["list"]),
        mesh=mesh,
        in_specs=(P("pass", None), P("list", None)),
        out_specs=(P("pass", "list"), P("list"), P("pass")),
        check_vma=False,
    )
```

```python
import functools
import math

import jax
import jax.numpy as jnp
from jax import lax
from jax.experimental import pallas as pl
from jax.experimental.pallas import tpu as pltpu
from jax.sharding import PartitionSpec as P

ITERS = 4
INV_TEMP = 20.0
LOG2E = math.log2(math.e)
LN2 = math.log(2.0)
F32 = jnp.float32
BF16 = jnp.bfloat16
MESH = pl.DeviceIdType.MESH
CHUNK = 512
GROUP = 256
STEP = 8
NA = 16
PARTS = 1
LAST_ORDER = (3, 2, 1)
LINKS = (4, 12, 1, 3)
ORDERS = ((0, 1, 2, 3), (1, 0, 3, 2), (2, 3, 0, 1), (3, 2, 1, 0))


def flip(index, bits):
    out = index
    b = 1
    while b <= bits:
        if bits & b:
            out = out + b * (1 - 2 * ((index // b) % 2))
        b *= 2
    return out


def place_of(order):
    first = order[0]
    axis_bits = lambda seq, unit: [0, unit * seq[1], unit * seq[0], unit * (seq[0] ^ seq[1])]
    low = {0: 1, 1: 3, 2: 1, 3: 3}
    unit = {0: 4, 1: 4, 2: 1, 3: 1}
    major = axis_bits((low[order[0]], low[order[1]]), unit[first])
    minor = axis_bits((low[order[2]], low[order[3]]), unit[order[2]])
    return [a + b for a in major for b in minor]


PLACES = [place_of(order) for order in ORDERS]


def chains(values, op, count=4):
    heads = list(values[:count])
    for i, value in enumerate(values[count:]):
        heads[i % count] = op(heads[i % count], value)
    return tree(heads, op)


def tree(values, op):
    while len(values) > 1:
        values = [op(values[i], values[i + 1]) for i in range(0, len(values), 2)]
    return values[0]


def lse2(values):
    top = tree(values, jnp.maximum)
    total = tree([jnp.exp2(v - top) for v in values], lax.add)
    return top + jnp.log(total) * LOG2E


def ring_hops(bits, size):
    return max(min(abs((i ^ bits) - i), size - abs((i ^ bits) - i)) for i in range(size))


PASS_ORDER = sorted(range(1, 16), key=lambda k: -ring_hops(k // 4, 4) - ring_hops(k % 4, 4))
Z_ORDER = sorted(range(1, 8), key=lambda k: -ring_hops(k, 8))
LIST_ORDER = sorted(range(1, 16), key=lambda k: -ring_hops(k // 2, 8))


def kernel(
    share, na,
    pas_hbm, cen_hbm,
    out_ref, cp_ref, rp_ref,
    cen, pas, tile, gain, pas_t, wts, stag, rb0, rb1, rb2,
    lane_a, lane_b, lane_c, racc, csrc, cslot, asrc, apair, amid, aslot, bsrc, bslot,
    u_ref, w_ref, m_ref, cfac, in_sem, cs, cr, ps, pr, zs, zr, bs, br, ss, sr,
):
    rows, depth = pas.shape
    lists = cen.shape[0]
    nrow, ncol = rows // 128, lists // 128
    nhalf = ncol // PARTS
    p, l = lax.axis_index("pass"), lax.axis_index("list")
    add = lambda values: tree(values, lax.add)

    loads = [pltpu.make_async_copy(cen_hbm, cen, in_sem.at[0])]
    for b in range(rows // CHUNK):
        part = pl.ds(b * CHUNK, CHUNK)
        loads.append(pltpu.make_async_copy(pas_hbm.at[part], pas.at[part], in_sem.at[b + 1]))
    for load in loads:
        load.start()

    barrier = pltpu.get_barrier_semaphore()
    for k in PASS_ORDER:
        pl.semaphore_signal(barrier, inc=1, device_id=(flip(p, k), l), device_id_type=MESH)
    for k in LIST_ORDER:
        pl.semaphore_signal(barrier, inc=1, device_id=(p, flip(l, k)), device_id_type=MESH)

    def col_send(i, h):
        for k in PASS_ORDER:
            pltpu.make_async_remote_copy(
                src_ref=csrc.at[i, h], dst_ref=cslot.at[i, h, k - 1], send_sem=cs,
                recv_sem=cr.at[i, h], device_id=(flip(p, k), l), device_id_type=MESH,
            ).start()

    def col_recv(i, h):
        pltpu.make_async_copy(cslot.at[i, h], cslot.at[i, h], cr.at[i, h]).wait()
        return [csrc[i, h]] + [cslot[i, h, k] for k in range(15)]

    def a_pair(i):
        return pltpu.make_async_remote_copy(
            src_ref=asrc.at[i], dst_ref=apair.at[i], send_sem=ps, recv_sem=pr.at[i],
            device_id=(p, flip(l, 1)), device_id_type=MESH,
        )

    def a_send(i, combine):
        a_pair(i).wait_recv()
        amid[i] = combine([asrc[i], apair[i]])
        for k in Z_ORDER:
            pltpu.make_async_remote_copy(
                src_ref=amid.at[i], dst_ref=aslot.at[i, k - 1], send_sem=zs, recv_sem=zr.at[i],
                device_id=(p, flip(l, 2 * k)), device_id_type=MESH,
            ).start()

    def a_recv(i, combine):
        pltpu.make_async_copy(aslot.at[i], aslot.at[i], zr.at[i]).wait()
        return combine([amid[i]] + [aslot[i, k] for k in range(7)])

    def b_send(i):
        for k in LIST_ORDER:
            pltpu.make_async_remote_copy(
                src_ref=bsrc.at[i], dst_ref=bslot.at[i, k - 1], send_sem=bs, recv_sem=br.at[i],
                device_id=(p, flip(l, k)), device_id_type=MESH,
            ).start()

    def b_recv(i, combine):
        pltpu.make_async_copy(bslot.at[i], bslot.at[i], br.at[i]).wait()
        return combine([bsrc[i]] + [bslot[i, k] for k in range(15)])

    def loop(first, last, body):
        def step(i, carry):
            body(i)
            return carry

        lax.fori_loop(first, last, step, 0)

    def unrolled(first, last, body):
        for i in range(first, last):
            body(i)

    def send_rows(i, combine, sweep):
        def part(ref, first):
            def body(b):
                for c, value in enumerate(sweep(b)):
                    ref[i, b * STEP + c - first:b * STEP + c - first + 1, :] = value

            return body

        unrolled(0, na // STEP, part(asrc, 0))
        a_pair(i).start()
        unrolled(na // STEP, nrow // STEP, part(bsrc, na))
        b_send(i)
        a_send(i, combine)

    part_a, part_b = slice(0, na), slice(na, nrow)

    def spread(values, h):
        for k in range(nhalf):
            at = pl.multiple_of((h * nhalf + k) * 128, 128)
            lane_b[pl.ds(at, 128), :] = jnp.broadcast_to(values[k:k + 1, :], (128, 128)).T

    def fold(i, h, ref):
        for k in range(nhalf):
            at = pl.multiple_of((h * nhalf + k) * 128, 128)
            csrc[i, h, k:k + 1, :] = jnp.sum(ref[pl.ds(at, 128), :].T, axis=0, keepdims=True)

    loads[0].wait()

    def logits(b):
        part = slice(b * CHUNK, (b + 1) * CHUNK)
        loads[b + 1].wait()
        tile[:, part] = lax.dot_general(
            cen[...], pas[part, :], (((1,), (1,)), ((), ())), preferred_element_type=F32
        ) * (INV_TEMP * LOG2E)

    def col_first(b):
        def body(r, carry):
            base = pl.ds(pl.multiple_of(r * 8, 8), 8)
            parts = [tile[base, c * 128:(c + 1) * 128] for c in range(b * CHUNK // 128, (b + 1) * CHUNK // 128)]
            top = tree(parts, jnp.maximum)
            if b > 0:
                top = jnp.maximum(top, lane_a[base, :])
            total = tree([jnp.exp2(part - top) for part in parts], lax.add)
            if b > 0:
                total = total + lane_b[base, :] * jnp.exp2(lane_a[base, :] - top)
            lane_a[base, :] = top
            lane_b[base, :] = total
            return carry

        lax.fori_loop(0, lists // 8, body, 0, unroll=96)

    logits(0)
    for b in range(1, rows // CHUNK):
        logits(b)
        col_first(b - 1)
    col_first(rows // CHUNK - 1)

    def col_first_send(h):
        for k in range(nhalf):
            at = pl.ds(pl.multiple_of((h * nhalf + k) * 128, 128), 128)
            tops = lane_a[at, :].T
            sums = lane_b[at, :].T
            top = jnp.max(tops, axis=0, keepdims=True)
            total = jnp.sum(sums * jnp.exp2(tops - top), axis=0, keepdims=True)
            csrc[0, h, k:k + 1, :] = top + jnp.log(total) * LOG2E
        col_send(0, h)

    pl.semaphore_wait(barrier, 30)
    loop(0, PARTS, col_first_send)

    def turn(b):
        part = pl.ds(pl.multiple_of(b * CHUNK, CHUNK), CHUNK)
        pas_t[:, :, part] = pas[part, :].T.reshape(16, depth // 16, CHUNK)

    loop(0, rows // CHUNK, turn)
    for h in range(PARTS):
        col_pot = share * LOG2E - lse2(col_recv(0, h))
        cp_ref[h * nhalf:(h + 1) * nhalf, :] = col_pot * LN2
        spread(col_pot, h)

    def columns(b):
        return [slice((b * STEP + c) * 128, (b * STEP + c + 1) * 128) for c in range(STEP)]

    def row_first(b):
        cols = columns(b)

        def row_top(r, tops):
            out = []
            for j in range(2):
                base = pl.ds(pl.multiple_of(r * 16, 16) + 8 * j, 8)
                pot = lane_b[base, :]
                out += [jnp.maximum(top, tile[base, col] + pot)
                        for top, col in zip(tops[j * STEP:(j + 1) * STEP], cols)]
            return tuple(out)

        tops = lax.fori_loop(
            0, lists // 16, row_top,
            tuple(jnp.full((8, 128), -jnp.inf, F32) for _ in range(2 * STEP)), unroll=8,
        )
        tops = [jnp.max(jnp.maximum(tops[c], tops[c + STEP]), axis=0, keepdims=True) for c in range(STEP)]
        wide = [jnp.broadcast_to(top, (8, 128)) for top in tops]

        def row_exp(r, sums):
            out = []
            for j in range(2):
                base = pl.ds(pl.multiple_of(r * 16, 16) + 8 * j, 8)
                pot = lane_b[base, :]
                for total, col, top in zip(sums[j * STEP:(j + 1) * STEP], cols, wide):
                    e = jnp.exp2(tile[base, col] + pot - top)
                    gain[base, col] = e
                    out.append(total + e)
            return tuple(out)

        sums = lax.fori_loop(
            0, lists // 16, row_exp, tuple(jnp.zeros((8, 128), F32) for _ in range(2 * STEP)), unroll=8
        )
        result = []
        for c, top in enumerate(tops):
            total = jnp.sum(sums[c] + sums[c + STEP], axis=0, keepdims=True)
            m_ref[pl.ds(b * STEP + c, 1), :] = top
            result.append(top + jnp.log(total) * LOG2E)
        return result

    send_rows(0, lse2, row_first)

    def first_factors(part, row_pot):
        rp_ref[part, :] = row_pot * LN2
        w_ref[part, :] = jnp.exp2(m_ref[part, :] + row_pot)
        u_ref[part, :] = w_ref[part, :]

    def next_factors(part, row_fac):
        u_ref[part, :] = w_ref[part, :] * row_fac
        m_ref[part, :] = row_fac

    def factors(part):
        return [jnp.broadcast_to(u_ref[c:c + 1, :], (8, 128)) for c in range(part.start, part.stop)]

    def col_sweep(part, first, count, out, start):
        us = factors(part)

        def body(r, carry):
            base = pl.ds(pl.multiple_of(first + r * 8, 8), 8)
            total = tree_sum([gain[base, c * 128:(c + 1) * 128] * us[c - part.start]
                              for c in range(part.start, part.stop)])
            out[base, :] = total if start is None else total + start[base, :]
            return carry

        lax.fori_loop(0, count // 8, body, 0, unroll=8)

    def row_sweep(b, h):
        cols = columns(b)

        def body(r, sums):
            out = []
            for j in range(2):
                base = pl.ds(pl.multiple_of(h * (lists // PARTS) + r * 16, 16) + 8 * j, 8)
                fac = lane_b[base, :]
                out += [total + gain[base, col] * fac
                        for total, col in zip(sums[j * STEP:(j + 1) * STEP], cols)]
            return tuple(out)

        sums = lax.fori_loop(
            0, lists // (16 * PARTS), body, tuple(jnp.zeros((8, 128), F32) for _ in range(2 * STEP)), unroll=8
        )
        return [sums[c] + sums[c + STEP] for c in range(STEP)], cols

    def plan(part, first, count, out, start):
        us = factors(part)

        def body(r):
            base = pl.multiple_of(first + r * 16, 16)
            low, high = pl.ds(base, 8), pl.ds(base + 8, 8)
            fac_low, fac_high = lane_b[low, :], lane_b[high, :]
            sums_low, sums_high = [], []
            for c in range(part.start, part.stop):
                col = slice(c * 128, (c + 1) * 128)
                a = gain[low, col] * us[c - part.start] * fac_low
                b = gain[high, col] * us[c - part.start] * fac_high
                sums_low.append(a)
                sums_high.append(b)
                wts[pl.ds(base, 16), col] = jnp.concatenate([a, b], axis=0).astype(BF16)
            sum_low, sum_high = tree_sum(sums_low), tree_sum(sums_high)
            out[low, :] = sum_low if start is None else sum_low + start[low, :]
            out[high, :] = sum_high if start is None else sum_high + start[high, :]

        loop(0, count // 16, body)

    first_factors(part_b, -b_recv(0, lse2))
    col_sweep(part_b, 0, lists, lane_a, None)
    first_factors(part_a, -a_recv(0, lse2))

    def iteration(step):
        def col_half(h):
            col_sweep(part_a, h * (lists // PARTS), lists // PARTS, lane_c, lane_a)
            fold(step, h, lane_c)
            col_send(step, h)

        loop(0, PARTS, col_half)
        for h in range(PARTS):
            col_fac = math.exp(share) / add(col_recv(step, h))
            cfac[h] = col_fac
            spread(col_fac, h)
            if h < PARTS - 1:
                def first_half(b):
                    sums, cols = row_sweep(b, 0)
                    for total, col in zip(sums, cols):
                        racc[:, col] = total

                unrolled(0, nrow // STEP, first_half)

        def last_half(b):
            sums, cols = row_sweep(b, PARTS - 1)
            return [
                jnp.sum(total + racc[:, col] if PARTS > 1 else total, axis=0, keepdims=True) * w_ref[pl.ds(b * STEP + c, 1), :]
                for c, (total, col) in enumerate(zip(sums, cols))
            ]

        send_rows(step, add, last_half)
        next_factors(part_b, 1.0 / b_recv(step, add))

        @pl.when(step < ITERS - 1)
        def _():
            col_sweep(part_b, 0, lists, lane_a, None)

        @pl.when(step == ITERS - 1)
        def _():
            plan(part_b, 0, lists, lane_a, None)

        next_factors(part_a, 1.0 / a_recv(step, add))

    loop(1, ITERS, iteration)

    half = depth // 32
    groups = lists // GROUP

    def hop(g, v, s):
        n = 8 >> s
        return pltpu.make_async_remote_copy(
            src_ref=stag.at[g, v, pl.ds(n, n)], dst_ref=(rb0, rb1)[s].at[g, v], send_sem=ss.at[s],
            recv_sem=sr.at[g, v, s], device_id=(flip(p, LINKS[ORDERS[v][s]]), l), device_id_type=MESH,
        )

    def group_sums(g):
        first = pl.multiple_of(g * GROUP, GROUP)
        plan(part_a, first, GROUP, lane_c, lane_a)
        w = wts[pl.ds(first, GROUP), :]
        left = jnp.concatenate([pas_t[flip(p, i)] for i in range(16)], axis=0)
        res = lax.dot_general(left, w, (((1,), (1,)), ((), ())), preferred_element_type=F32)
        for v in range(4):
            h, c = v // 2, v % 2
            for i in range(16):
                stag[g, v, PLACES[v].index(i)] = res[
                    (2 * i + h) * half:(2 * i + h + 1) * half, c * 128:(c + 1) * 128]
        for v in range(4):
            hop(g, v, 0).start()

    loop(0, groups, group_sums)

    def mass_half(h):
        fold(ITERS, h, lane_c)
        col_send(ITERS, h)

    loop(0, PARTS, mass_half)
    rp_ref[...] += jnp.log(m_ref[...])
    for h in range(PARTS):
        cp_ref[h * nhalf:(h + 1) * nhalf, :] += jnp.log(cfac[h])
    def second(g):
        for v in range(4):
            hop(g, v, 0).wait_recv()
            for i in range(4, 8):
                stag[g, v, i] += rb0[g, v, i]
            hop(g, v, 1).start()
            for i in range(4):
                stag[g, v, i] += rb0[g, v, i]

    def third(g):
        for v in range(4):
            hop(g, v, 1).wait_recv()
            for i in LAST_ORDER:
                stag[g, v, i] += rb1[g, v, i]
                pltpu.make_async_remote_copy(
                    src_ref=stag.at[g, v, i], dst_ref=rb2.at[g, v, i - 1], send_sem=ss.at[2],
                    recv_sem=sr.at[g, v, 2], device_id=(flip(p, PLACES[v][i]), l), device_id_type=MESH,
                ).start()
            stag[g, v, 0] += rb1[g, v, 0]

    loop(0, groups, second)
    loop(0, groups, third)
    mass = [add(col_recv(ITERS, h)) for h in range(PARTS)]
    for g in range(groups):
        for v in range(4):
            pltpu.make_async_copy(rb2.at[g, v], rb2.at[g, v], sr.at[g, v, 2]).wait()
            h, c = v // 2, v % 2
            at = g * (GROUP // 128) + c
            total = (stag[g, v, 0] + rb2[g, v, 0]) + (rb2[g, v, 1] + rb2[g, v, 2])
            out_ref[h * half:(h + 1) * half, at * 128:(at + 1) * 128] = (
                total / mass[at // nhalf][at % nhalf:at % nhalf + 1, :])

    for ref, sem in ((cslot, cs), (apair, ps), (aslot, zs), (bslot, bs)):
        pltpu.make_async_copy(ref, ref, sem).wait()
    for s, ref in enumerate((rb0, rb1, rb2)):
        pltpu.make_async_copy(ref, ref, ss.at[s]).wait()


def copy_out(*refs):
    n = len(refs) // 2
    for src, dst in zip(refs[:n], refs[n:]):
        dst[...] = src[...]


def tree_sum(values):
    values = list(values)
    while len(values) > 1:
        pairs = [values[i] + values[i + 1] for i in range(0, len(values) - 1, 2)]
        values = pairs + values[len(values) - len(values) % 2:]
    return values[0]


def local(n_pass, n_list, passages, centroids):
    rows, depth = passages.shape
    lists = centroids.shape[0]
    nrow, ncol = rows // 128, lists // 128
    na = NA
    share = math.log(rows * n_pass / (lists * n_list))
    groups, part = lists // GROUP, depth // 32
    dma = pltpu.SemaphoreType.DMA
    vmem = pltpu.VMEM
    shapes = (
        jax.ShapeDtypeStruct((depth // n_pass, lists), F32),
        jax.ShapeDtypeStruct((ncol, 128), F32),
        jax.ShapeDtypeStruct((nrow, 128), F32),
    )
    whole = pl.BlockSpec(memory_space=pltpu.VMEM)
    results = pl.pallas_call(
        functools.partial(kernel, share, na),
        out_shape=shapes,
        in_specs=[pl.BlockSpec(memory_space=pl.ANY)] * 2,
        out_specs=[whole] * 3,
        scratch_shapes=[
            vmem((lists, depth), BF16),
            vmem((rows, depth), BF16),
            vmem((lists, rows), F32),
            vmem((lists, rows), F32),
            vmem((16, depth // 16, rows), BF16),
            vmem((lists, rows), BF16),
            vmem((groups, 4, 16, part, 128), F32),
            vmem((groups, 4, 8, part, 128), F32),
            vmem((groups, 4, 4, part, 128), F32),
            vmem((groups, 4, 3, part, 128), F32),
            vmem((lists, 128), F32),
            vmem((lists, 128), F32),
            vmem((lists, 128), F32),
            vmem((8, rows), F32),
            vmem((ITERS + 1, PARTS, ncol // PARTS, 128), F32),
            vmem((ITERS + 1, PARTS, 15, ncol // PARTS, 128), F32),
            vmem((ITERS, na, 128), F32),
            vmem((ITERS, na, 128), F32),
            vmem((ITERS, na, 128), F32),
            vmem((ITERS, 7, na, 128), F32),
            vmem((ITERS, nrow - na, 128), F32),
            vmem((ITERS, 15, nrow - na, 128), F32),
            vmem((nrow, 128), F32),
            vmem((nrow, 128), F32),
            vmem((nrow, 128), F32),
            vmem((PARTS, ncol // PARTS, 128), F32),
            dma((1 + rows // CHUNK,)),
            dma, dma((ITERS + 1, PARTS)),
            dma, dma((ITERS,)),
            dma, dma((ITERS,)),
            dma, dma((ITERS,)),
            dma((3,)), dma((groups, 4, 3)),
        ],
        compiler_params=pltpu.CompilerParams(
            collective_id=0, has_side_effects=True, vmem_limit_bytes=56 << 20
        ),
        cost_estimate=pl.CostEstimate(
            flops=4 * rows * depth * lists, bytes_accessed=2 * (rows + lists) * depth,
            transcendentals=2 * rows * lists,
        ),
    )(passages, centroids)
    out, cp, rp = pl.pallas_call(
        copy_out, out_shape=shapes, in_specs=[whole] * 3, out_specs=[whole] * 3
    )(*results)
    return out, cp.reshape(lists), rp.reshape(rows)


def solution(mesh):
    return jax.shard_map(
        functools.partial(local, mesh.shape["pass"], mesh.shape["list"]),
        mesh=mesh,
        in_specs=(P("pass", None), P("list", None)),
        out_specs=(P("pass", "list"), P("list"), P("pass")),
        check_vma=False,
    )
```

```python
import functools
import math

import jax
import jax.numpy as jnp
from jax import lax
from jax.experimental import pallas as pl
from jax.experimental.pallas import tpu as pltpu
from jax.sharding import PartitionSpec as P

ITERS = 4
INV_TEMP = 20.0
LOG2E = math.log2(math.e)
LN2 = math.log(2.0)
F32 = jnp.float32
BF16 = jnp.bfloat16
MESH = pl.DeviceIdType.MESH
CHUNK = 512
GROUP = 256
STEP = 8
NA = 16
PARTS = 1
LAST_ORDER = (3, 2, 1)
LINKS = (4, 12, 1, 3)
ORDERS = ((0, 1, 2, 3), (1, 0, 3, 2), (2, 3, 0, 1), (3, 2, 1, 0))


def flip(index, bits):
    out = index
    b = 1
    while b <= bits:
        if bits & b:
            out = out + b * (1 - 2 * ((index // b) % 2))
        b *= 2
    return out


def place_of(order):
    first = order[0]
    axis_bits = lambda seq, unit: [0, unit * seq[1], unit * seq[0], unit * (seq[0] ^ seq[1])]
    low = {0: 1, 1: 3, 2: 1, 3: 3}
    unit = {0: 4, 1: 4, 2: 1, 3: 1}
    major = axis_bits((low[order[0]], low[order[1]]), unit[first])
    minor = axis_bits((low[order[2]], low[order[3]]), unit[order[2]])
    return [a + b for a in major for b in minor]


PLACES = [place_of(order) for order in ORDERS]


def chains(values, op, count=4):
    heads = list(values[:count])
    for i, value in enumerate(values[count:]):
        heads[i % count] = op(heads[i % count], value)
    return tree(heads, op)


def tree(values, op):
    while len(values) > 1:
        values = [op(values[i], values[i + 1]) for i in range(0, len(values), 2)]
    return values[0]


def lse2(values):
    top = tree(values, jnp.maximum)
    total = tree([jnp.exp2(v - top) for v in values], lax.add)
    return top + jnp.log(total) * LOG2E


def ring_hops(bits, size):
    return max(min(abs((i ^ bits) - i), size - abs((i ^ bits) - i)) for i in range(size))


PASS_ORDER = sorted(range(1, 16), key=lambda k: -ring_hops(k // 4, 4) - ring_hops(k % 4, 4))
Z_ORDER = sorted(range(1, 8), key=lambda k: -ring_hops(k, 8))
LIST_ORDER = sorted(range(1, 16), key=lambda k: -ring_hops(k // 2, 8))


def kernel(
    share, na,
    pas_hbm, cen_hbm,
    out_ref, cp_ref, rp_ref,
    cen, pas, tile, gain, pas_t, wts, stag, rb0, rb1, rb2,
    lane_a, lane_b, lane_c, racc, csrc, cslot, asrc, apair, amid, aslot, bsrc, bslot,
    u_ref, w_ref, m_ref, cfac, in_sem, cs, cr, ps, pr, zs, zr, bs, br, ss, sr,
):
    rows, depth = pas.shape
    lists = cen.shape[0]
    nrow, ncol = rows // 128, lists // 128
    nhalf = ncol // PARTS
    p, l = lax.axis_index("pass"), lax.axis_index("list")
    add = lambda values: tree(values, lax.add)

    loads = [pltpu.make_async_copy(cen_hbm, cen, in_sem.at[0])]
    for b in range(rows // CHUNK):
        part = pl.ds(b * CHUNK, CHUNK)
        loads.append(pltpu.make_async_copy(pas_hbm.at[part], pas.at[part], in_sem.at[b + 1]))
    for load in loads:
        load.start()

    barrier = pltpu.get_barrier_semaphore()
    for k in PASS_ORDER:
        pl.semaphore_signal(barrier, inc=1, device_id=(flip(p, k), l), device_id_type=MESH)
    for k in LIST_ORDER:
        pl.semaphore_signal(barrier, inc=1, device_id=(p, flip(l, k)), device_id_type=MESH)

    def col_send(i, h):
        for k in PASS_ORDER:
            pltpu.make_async_remote_copy(
                src_ref=csrc.at[i, h], dst_ref=cslot.at[i, h, k - 1], send_sem=cs,
                recv_sem=cr.at[i, h], device_id=(flip(p, k), l), device_id_type=MESH,
            ).start()

    def col_recv(i, h):
        pltpu.make_async_copy(cslot.at[i, h], cslot.at[i, h], cr.at[i, h]).wait()
        return [csrc[i, h]] + [cslot[i, h, k] for k in range(15)]

    def a_pair(i):
        return pltpu.make_async_remote_copy(
            src_ref=asrc.at[i], dst_ref=apair.at[i], send_sem=ps, recv_sem=pr.at[i],
            device_id=(p, flip(l, 1)), device_id_type=MESH,
        )

    def a_send(i, combine):
        a_pair(i).wait_recv()
        amid[i] = combine([asrc[i], apair[i]])
        for k in Z_ORDER:
            pltpu.make_async_remote_copy(
                src_ref=amid.at[i], dst_ref=aslot.at[i, k - 1], send_sem=zs, recv_sem=zr.at[i],
                device_id=(p, flip(l, 2 * k)), device_id_type=MESH,
            ).start()

    def a_recv(i, combine):
        pltpu.make_async_copy(aslot.at[i], aslot.at[i], zr.at[i]).wait()
        return combine([amid[i]] + [aslot[i, k] for k in range(7)])

    def b_send(i):
        for k in LIST_ORDER:
            pltpu.make_async_remote_copy(
                src_ref=bsrc.at[i], dst_ref=bslot.at[i, k - 1], send_sem=bs, recv_sem=br.at[i],
                device_id=(p, flip(l, k)), device_id_type=MESH,
            ).start()

    def b_recv(i, combine):
        pltpu.make_async_copy(bslot.at[i], bslot.at[i], br.at[i]).wait()
        return combine([bsrc[i]] + [bslot[i, k] for k in range(15)])

    def loop(first, last, body):
        def step(i, carry):
            body(i)
            return carry

        lax.fori_loop(first, last, step, 0)

    def unrolled(first, last, body):
        for i in range(first, last):
            body(i)

    def send_rows(i, combine, sweep):
        def part(ref, first):
            def body(b):
                for c, value in enumerate(sweep(b)):
                    ref[i, b * STEP + c - first:b * STEP + c - first + 1, :] = value

            return body

        unrolled(0, na // STEP, part(asrc, 0))
        a_pair(i).start()
        unrolled(na // STEP, nrow // STEP, part(bsrc, na))
        b_send(i)
        a_send(i, combine)

    part_a, part_b = slice(0, na), slice(na, nrow)

    def spread(values, h):
        for k in range(nhalf):
            at = pl.multiple_of((h * nhalf + k) * 128, 128)
            lane_b[pl.ds(at, 128), :] = jnp.broadcast_to(values[k:k + 1, :], (128, 128)).T

    def fold(i, h, ref):
        for k in range(nhalf):
            at = pl.multiple_of((h * nhalf + k) * 128, 128)
            csrc[i, h, k:k + 1, :] = jnp.sum(ref[pl.ds(at, 128), :].T, axis=0, keepdims=True)

    loads[0].wait()

    def logits(b):
        part = slice(b * CHUNK, (b + 1) * CHUNK)
        loads[b + 1].wait()
        tile[:, part] = lax.dot_general(
            cen[...], pas[part, :], (((1,), (1,)), ((), ())), preferred_element_type=F32
        ) * (INV_TEMP * LOG2E)

    def col_first(b):
        def body(r, carry):
            base = pl.ds(pl.multiple_of(r * 8, 8), 8)
            parts = [tile[base, c * 128:(c + 1) * 128] for c in range(b * CHUNK // 128, (b + 1) * CHUNK // 128)]
            top = tree(parts, jnp.maximum)
            if b > 0:
                top = jnp.maximum(top, lane_a[base, :])
            total = tree([jnp.exp2(part - top) for part in parts], lax.add)
            if b > 0:
                total = total + lane_b[base, :] * jnp.exp2(lane_a[base, :] - top)
            lane_a[base, :] = top
            lane_b[base, :] = total
            return carry

        lax.fori_loop(0, lists // 8, body, 0, unroll=96)

    logits(0)
    for b in range(1, rows // CHUNK):
        logits(b)
        col_first(b - 1)
    col_first(rows // CHUNK - 1)

    def col_first_send(h):
        for k in range(nhalf):
            at = pl.ds(pl.multiple_of((h * nhalf + k) * 128, 128), 128)
            tops = lane_a[at, :].T
            sums = lane_b[at, :].T
            top = jnp.max(tops, axis=0, keepdims=True)
            total = jnp.sum(sums * jnp.exp2(tops - top), axis=0, keepdims=True)
            csrc[0, h, k:k + 1, :] = top + jnp.log(total) * LOG2E
        col_send(0, h)

    pl.semaphore_wait(barrier, 30)
    loop(0, PARTS, col_first_send)

    def turn(b):
        part = pl.ds(pl.multiple_of(b * CHUNK, CHUNK), CHUNK)
        pas_t[:, :, part] = pas[part, :].T.reshape(16, depth // 16, CHUNK)

    loop(0, rows // CHUNK, turn)
    for h in range(PARTS):
        col_pot = share * LOG2E - lse2(col_recv(0, h))
        cp_ref[h * nhalf:(h + 1) * nhalf, :] = col_pot * LN2
        spread(col_pot, h)

    def columns(b):
        return [slice((b * STEP + c) * 128, (b * STEP + c + 1) * 128) for c in range(STEP)]

    def row_first(b):
        cols = columns(b)

        def row_top(r, tops):
            out = []
            for j in range(2):
                base = pl.ds(pl.multiple_of(r * 16, 16) + 8 * j, 8)
                pot = lane_b[base, :]
                out += [jnp.maximum(top, tile[base, col] + pot)
                        for top, col in zip(tops[j * STEP:(j + 1) * STEP], cols)]
            return tuple(out)

        tops = lax.fori_loop(
            0, lists // 16, row_top,
            tuple(jnp.full((8, 128), -jnp.inf, F32) for _ in range(2 * STEP)), unroll=16,
        )
        tops = [jnp.max(jnp.maximum(tops[c], tops[c + STEP]), axis=0, keepdims=True) for c in range(STEP)]
        wide = [jnp.broadcast_to(top, (8, 128)) for top in tops]

        def row_exp(r, sums):
            out = []
            for j in range(2):
                base = pl.ds(pl.multiple_of(r * 16, 16) + 8 * j, 8)
                pot = lane_b[base, :]
                for total, col, top in zip(sums[j * STEP:(j + 1) * STEP], cols, wide):
                    e = jnp.exp2(tile[base, col] + pot - top)
                    gain[base, col] = e
                    out.append(total + e)
            return tuple(out)

        sums = lax.fori_loop(
            0, lists // 16, row_exp, tuple(jnp.zeros((8, 128), F32) for _ in range(2 * STEP)), unroll=16
        )
        result = []
        for c, top in enumerate(tops):
            total = jnp.sum(sums[c] + sums[c + STEP], axis=0, keepdims=True)
            m_ref[pl.ds(b * STEP + c, 1), :] = top
            result.append(top + jnp.log(total) * LOG2E)
        return result

    send_rows(0, lse2, row_first)

    def first_factors(part, row_pot):
        rp_ref[part, :] = row_pot * LN2
        w_ref[part, :] = jnp.exp2(m_ref[part, :] + row_pot)
        u_ref[part, :] = w_ref[part, :]

    def next_factors(part, row_fac):
        u_ref[part, :] = w_ref[part, :] * row_fac
        m_ref[part, :] = row_fac

    def factors(part):
        return [jnp.broadcast_to(u_ref[c:c + 1, :], (8, 128)) for c in range(part.start, part.stop)]

    def col_sweep(part, first, count, out, start):
        us = factors(part)

        def body(r, carry):
            base = pl.ds(pl.multiple_of(first + r * 8, 8), 8)
            total = tree_sum([gain[base, c * 128:(c + 1) * 128] * us[c - part.start]
                              for c in range(part.start, part.stop)])
            out[base, :] = total if start is None else total + start[base, :]
            return carry

        lax.fori_loop(0, count // 8, body, 0, unroll=16)

    def row_sweep(b, h):
        cols = columns(b)

        def body(r, sums):
            out = []
            for j in range(2):
                base = pl.ds(pl.multiple_of(h * (lists // PARTS) + r * 16, 16) + 8 * j, 8)
                fac = lane_b[base, :]
                out += [total + gain[base, col] * fac
                        for total, col in zip(sums[j * STEP:(j + 1) * STEP], cols)]
            return tuple(out)

        sums = lax.fori_loop(
            0, lists // (16 * PARTS), body, tuple(jnp.zeros((8, 128), F32) for _ in range(2 * STEP)), unroll=16
        )
        return [sums[c] + sums[c + STEP] for c in range(STEP)], cols

    def plan(part, first, count, out, start):
        us = factors(part)

        def body(r):
            base = pl.multiple_of(first + r * 16, 16)
            low, high = pl.ds(base, 8), pl.ds(base + 8, 8)
            fac_low, fac_high = lane_b[low, :], lane_b[high, :]
            sums_low, sums_high = [], []
            for c in range(part.start, part.stop):
                col = slice(c * 128, (c + 1) * 128)
                a = gain[low, col] * us[c - part.start] * fac_low
                b = gain[high, col] * us[c - part.start] * fac_high
                sums_low.append(a)
                sums_high.append(b)
                wts[pl.ds(base, 16), col] = jnp.concatenate([a, b], axis=0).astype(BF16)
            sum_low, sum_high = tree_sum(sums_low), tree_sum(sums_high)
            out[low, :] = sum_low if start is None else sum_low + start[low, :]
            out[high, :] = sum_high if start is None else sum_high + start[high, :]

        loop(0, count // 16, body)

    first_factors(part_b, -b_recv(0, lse2))
    col_sweep(part_b, 0, lists, lane_a, None)
    first_factors(part_a, -a_recv(0, lse2))

    def iteration(step):
        def col_half(h):
            col_sweep(part_a, h * (lists // PARTS), lists // PARTS, lane_c, lane_a)
            fold(step, h, lane_c)
            col_send(step, h)

        loop(0, PARTS, col_half)
        for h in range(PARTS):
            col_fac = math.exp(share) / add(col_recv(step, h))
            cfac[h] = col_fac
            spread(col_fac, h)
            if h < PARTS - 1:
                def first_half(b):
                    sums, cols = row_sweep(b, 0)
                    for total, col in zip(sums, cols):
                        racc[:, col] = total

                unrolled(0, nrow // STEP, first_half)

        def last_half(b):
            sums, cols = row_sweep(b, PARTS - 1)
            return [
                jnp.sum(total + racc[:, col] if PARTS > 1 else total, axis=0, keepdims=True) * w_ref[pl.ds(b * STEP + c, 1), :]
                for c, (total, col) in enumerate(zip(sums, cols))
            ]

        send_rows(step, add, last_half)
        next_factors(part_b, 1.0 / b_recv(step, add))

        @pl.when(step < ITERS - 1)
        def _():
            col_sweep(part_b, 0, lists, lane_a, None)

        @pl.when(step == ITERS - 1)
        def _():
            plan(part_b, 0, lists, lane_a, None)

        next_factors(part_a, 1.0 / a_recv(step, add))

    loop(1, ITERS, iteration)

    half = depth // 32
    groups = lists // GROUP

    def hop(g, v, s):
        n = 8 >> s
        return pltpu.make_async_remote_copy(
            src_ref=stag.at[g, v, pl.ds(n, n)], dst_ref=(rb0, rb1)[s].at[g, v], send_sem=ss.at[s],
            recv_sem=sr.at[g, v, s], device_id=(flip(p, LINKS[ORDERS[v][s]]), l), device_id_type=MESH,
        )

    def group_sums(g):
        first = pl.multiple_of(g * GROUP, GROUP)
        plan(part_a, first, GROUP, lane_c, lane_a)
        w = wts[pl.ds(first, GROUP), :]
        left = jnp.concatenate([pas_t[flip(p, i)] for i in range(16)], axis=0)
        res = lax.dot_general(left, w, (((1,), (1,)), ((), ())), preferred_element_type=F32)
        for v in range(4):
            h, c = v // 2, v % 2
            for i in range(16):
                stag[g, v, PLACES[v].index(i)] = res[
                    (2 * i + h) * half:(2 * i + h + 1) * half, c * 128:(c + 1) * 128]
        for v in range(4):
            hop(g, v, 0).start()

    loop(0, groups, group_sums)

    def mass_half(h):
        fold(ITERS, h, lane_c)
        col_send(ITERS, h)

    loop(0, PARTS, mass_half)
    rp_ref[...] += jnp.log(m_ref[...])
    for h in range(PARTS):
        cp_ref[h * nhalf:(h + 1) * nhalf, :] += jnp.log(cfac[h])
    def second(g):
        for v in range(4):
            hop(g, v, 0).wait_recv()
            for i in range(4, 8):
                stag[g, v, i] += rb0[g, v, i]
            hop(g, v, 1).start()
            for i in range(4):
                stag[g, v, i] += rb0[g, v, i]

    def third(g):
        for v in range(4):
            hop(g, v, 1).wait_recv()
            for i in LAST_ORDER:
                stag[g, v, i] += rb1[g, v, i]
                pltpu.make_async_remote_copy(
                    src_ref=stag.at[g, v, i], dst_ref=rb2.at[g, v, i - 1], send_sem=ss.at[2],
                    recv_sem=sr.at[g, v, 2], device_id=(flip(p, PLACES[v][i]), l), device_id_type=MESH,
                ).start()
            stag[g, v, 0] += rb1[g, v, 0]

    loop(0, groups, second)
    loop(0, groups, third)
    mass = [add(col_recv(ITERS, h)) for h in range(PARTS)]
    for g in range(groups):
        for v in range(4):
            pltpu.make_async_copy(rb2.at[g, v], rb2.at[g, v], sr.at[g, v, 2]).wait()
            h, c = v // 2, v % 2
            at = g * (GROUP // 128) + c
            total = (stag[g, v, 0] + rb2[g, v, 0]) + (rb2[g, v, 1] + rb2[g, v, 2])
            out_ref[h * half:(h + 1) * half, at * 128:(at + 1) * 128] = (
                total / mass[at // nhalf][at % nhalf:at % nhalf + 1, :])

    for ref, sem in ((cslot, cs), (apair, ps), (aslot, zs), (bslot, bs)):
        pltpu.make_async_copy(ref, ref, sem).wait()
    for s, ref in enumerate((rb0, rb1, rb2)):
        pltpu.make_async_copy(ref, ref, ss.at[s]).wait()


def copy_out(*refs):
    n = len(refs) // 2
    for src, dst in zip(refs[:n], refs[n:]):
        dst[...] = src[...]


def tree_sum(values):
    values = list(values)
    while len(values) > 1:
        pairs = [values[i] + values[i + 1] for i in range(0, len(values) - 1, 2)]
        values = pairs + values[len(values) - len(values) % 2:]
    return values[0]


def local(n_pass, n_list, passages, centroids):
    rows, depth = passages.shape
    lists = centroids.shape[0]
    nrow, ncol = rows // 128, lists // 128
    na = NA
    share = math.log(rows * n_pass / (lists * n_list))
    groups, part = lists // GROUP, depth // 32
    dma = pltpu.SemaphoreType.DMA
    vmem = pltpu.VMEM
    shapes = (
        jax.ShapeDtypeStruct((depth // n_pass, lists), F32),
        jax.ShapeDtypeStruct((ncol, 128), F32),
        jax.ShapeDtypeStruct((nrow, 128), F32),
    )
    whole = pl.BlockSpec(memory_space=pltpu.VMEM)
    results = pl.pallas_call(
        functools.partial(kernel, share, na),
        out_shape=shapes,
        in_specs=[pl.BlockSpec(memory_space=pl.ANY)] * 2,
        out_specs=[whole] * 3,
        scratch_shapes=[
            vmem((lists, depth), BF16),
            vmem((rows, depth), BF16),
            vmem((lists, rows), F32),
            vmem((lists, rows), F32),
            vmem((16, depth // 16, rows), BF16),
            vmem((lists, rows), BF16),
            vmem((groups, 4, 16, part, 128), F32),
            vmem((groups, 4, 8, part, 128), F32),
            vmem((groups, 4, 4, part, 128), F32),
            vmem((groups, 4, 3, part, 128), F32),
            vmem((lists, 128), F32),
            vmem((lists, 128), F32),
            vmem((lists, 128), F32),
            vmem((8, rows), F32),
            vmem((ITERS + 1, PARTS, ncol // PARTS, 128), F32),
            vmem((ITERS + 1, PARTS, 15, ncol // PARTS, 128), F32),
            vmem((ITERS, na, 128), F32),
            vmem((ITERS, na, 128), F32),
            vmem((ITERS, na, 128), F32),
            vmem((ITERS, 7, na, 128), F32),
            vmem((ITERS, nrow - na, 128), F32),
            vmem((ITERS, 15, nrow - na, 128), F32),
            vmem((nrow, 128), F32),
            vmem((nrow, 128), F32),
            vmem((nrow, 128), F32),
            vmem((PARTS, ncol // PARTS, 128), F32),
            dma((1 + rows // CHUNK,)),
            dma, dma((ITERS + 1, PARTS)),
            dma, dma((ITERS,)),
            dma, dma((ITERS,)),
            dma, dma((ITERS,)),
            dma((3,)), dma((groups, 4, 3)),
        ],
        compiler_params=pltpu.CompilerParams(
            collective_id=0, has_side_effects=True, vmem_limit_bytes=60 << 20
        ),
        cost_estimate=pl.CostEstimate(
            flops=4 * rows * depth * lists, bytes_accessed=2 * (rows + lists) * depth,
            transcendentals=2 * rows * lists,
        ),
    )(passages, centroids)
    out, cp, rp = pl.pallas_call(
        copy_out, out_shape=shapes, in_specs=[whole] * 3, out_specs=[whole] * 3
    )(*results)
    return out, cp.reshape(lists), rp.reshape(rows)


def solution(mesh):
    return jax.shard_map(
        functools.partial(local, mesh.shape["pass"], mesh.shape["list"]),
        mesh=mesh,
        in_specs=(P("pass", None), P("list", None)),
        out_specs=(P("pass", "list"), P("list"), P("pass")),
        check_vma=False,
    )
```
